32 devices in a mesh: grp: 4 (over y, x), feat: 8 (over z, core).
Axes of the slice: x: 2, y: 2, z: 4, core: 2. Of those that a mesh axis runs over, the one named last changes fastest.
Arguments:
- points: bfloat16 [8192, 32], P(('grp', 'feat')), may hold values from -6 to 6
- dual_weights: float32 [8192, 64], P(('grp', 'feat')), may hold values from -6 to 6
- velocity: float32 [8192, 64], P(('grp', 'feat')), may hold values from -1.75 to 1.75
- observed: float32 [8192], P(('grp', 'feat')), may hold values from -12 to 12
- noise_draws: float32 [8192, 64], P(('grp', 'feat')), may hold values from -3 to 3
- frequencies: bfloat16 [32, 16384], P(None, 'feat'), may hold values from -1.5 to 1.5
- phases: float32 [16384], P('feat'), may hold values from 0 to 6.2832
- prior_weights: bfloat16 [16384, 64], P('feat'), may hold values from -6 to 6
- batch_tiles: int32 [2, 4, 1], P(None, 'grp'), may hold values from 0 to 15, as said below
Outputs:
- new_duals: float32 [8192, 64], P(('grp', 'feat'))
- new_velocity: float32 [8192, 64], P(('grp', 'feat'))
The draws below stay inside these ranges and needn't reach their ends.
Inputs may be any that keep to these rules, and one draw needn't show every extreme that they name: `batch_tiles`: in each step the 1 tile numbers of a group are distinct.
All inputs are finite; a program needn't handle non-finite values.
Results may differ from the reference program's by a relative error of at most 0.0012.
Values may be sent and summed in bfloat16 or wider, within the bound.
No kernel may reach another device: no remote copies, remote signals or barrier semaphores. Data moves between devices by JAX's collectives and lax.ppermute only.
A program may use at most 64 MiB of HBM per device.

```python
import math
import jax
import jax.numpy as jnp
from jax import lax

D = 32
RFF = 16384
SAMPLES = 64
NPT = 256
TILE = 128
TILES_G = 1
STEPS = 2
GROUP_PTS = 2048
GROUP_TILES = 16
POINTS = 8192
BATCH = 512
N_GRP = 4
DEVICES = 32


def place_value(chosen_row, slot_index, target_value):
    where_at = jnp.argmax(chosen_row == target_value)
    other_value = chosen_row[slot_index]
    return chosen_row.at[where_at].set(other_value).at[slot_index].set(target_value)


def draw_batch_tiles(key, part):
    group_total = BATCH // (TILES_G * TILE)
    subkeys = jax.random.split(key, STEPS * group_total)
    shuffled = jax.vmap(lambda subkey: jax.random.permutation(subkey, GROUP_TILES))(subkeys).astype(jnp.int32)
    first_group = jax.random.randint(jax.random.fold_in(key, 11), (), 0, group_total)
    first_slot = jax.random.randint(jax.random.fold_in(key, 12), (), 0, TILES_G)
    second_group = jax.random.randint(jax.random.fold_in(key, 13), (), 0, group_total) + group_total * (STEPS - 1)
    second_slot = jax.random.randint(jax.random.fold_in(key, 14), (), 0, TILES_G)
    shuffled = shuffled.at[first_group].set(place_value(shuffled[first_group], first_slot, GROUP_TILES - 1))
    shuffled = shuffled.at[second_group].set(place_value(shuffled[second_group], second_slot, 0))
    return shuffled[:, :TILES_G].reshape(STEPS, group_total, TILES_G).astype(jnp.int32)


def draw_points(key, part):
    label_key = jax.random.fold_in(key, 21)
    center_key = jax.random.fold_in(key, 22)
    spread_key = jax.random.fold_in(key, 23)
    labels = jax.random.randint(label_key, (POINTS,), 0, 4).astype(jnp.int32)
    centers = 1.1 * jax.random.normal(center_key, (4, D), jnp.float32)
    spread = 0.8 * jax.random.normal(spread_key, (POINTS, D), jnp.float32)
    values = jnp.clip(centers[labels] + spread, -6.0, 6.0)
    return values.astype(jnp.bfloat16)


def levels(own_key, extent, pieces, least, largest):
    factor_of = 1.0
    for position, blocks in pieces:
        steps = jax.random.uniform(jax.random.fold_in(jax.random.fold_in(own_key, 6), position), (blocks,), jnp.float32, least / len(pieces), largest / len(pieces))
        factor_of = factor_of * jnp.repeat(jnp.exp(steps), extent[position] // blocks).reshape((-1,) + (1,) * (len(extent) - 1 - position))
    return factor_of


def centred(key, dims, deviation, reach, cuts=(), kind=jnp.bfloat16):
    values = jax.random.normal(key, dims, jnp.float32) * deviation
    if len(cuts) > 0:
        values = levels(key, dims, cuts, -0.22, 0.18) * values
    return jnp.clip(values, min=-reach, max=reach).astype(kind)


def setup_inputs(seed: int = 0) -> dict:
    key_of = jax.random.split(jax.random.key(seed), 10)
    points = draw_points(jax.random.fold_in(key_of[9], 71), 0)
    dual_weights = centred(key_of[1], (POINTS, SAMPLES), 1.0, 6.0, ((0, 32),), jnp.float32)
    velocity = centred(key_of[2], (POINTS, SAMPLES), 0.3, 1.75, ((0, 32),), jnp.float32)
    observed = centred(key_of[3], (POINTS,), 2.0, 12.0, ((0, 32),), jnp.float32)
    noise_draws = centred(key_of[4], (POINTS, SAMPLES), 0.5, 3.0, ((0, 32),), jnp.float32)
    frequencies = centred(key_of[5], (D, RFF), ((2 / D) ** 0.5), 1.5, ((1, 8),))
    phases = jnp.clip(6.2832 * jax.random.uniform(key_of[6], (RFF,), jnp.float32) ** levels(key_of[6], (RFF,), ((0, 8),), -0.2, 0.2), 0.0, 6.2832)
    prior_weights = centred(key_of[7], (RFF, SAMPLES), 1.0, 6.0, ((0, 8),))
    batch_tiles = draw_batch_tiles(jax.random.fold_in(key_of[9], 71), 0)
    return {"points": points, "dual_weights": dual_weights, "velocity": velocity, "observed": observed, "noise_draws": noise_draws, "frequencies": frequencies, "phases": phases, "prior_weights": prior_weights, "batch_tiles": batch_tiles}


amplitude = 4.0
signal = 2.0
momentum = 0.9
step_size = 0.5

def kernel_values(picked, point_block, norm_block):
    row_sq = lax.optimization_barrier(jnp.sum(jnp.square(picked.astype(jnp.float32)), axis=1))
    inner_prod = lax.dot_general(picked, point_block, (((1,), (1,)), ((), ())), preferred_element_type=jnp.float32)
    distance = row_sq[:, None] + norm_block[None, :] - 2.0 * inner_prod
    return (amplitude * jnp.exp(-distance / point_block.shape[1])).astype(jnp.bfloat16)

def reference(points, dual_weights, velocity, observed, noise_draws, frequencies, phases, prior_weights, batch_tiles):
    inv_root = 1.0 / math.sqrt(POINTS)
    prior_scale = signal * math.sqrt(2.0 / RFF)
    norm_all = lax.optimization_barrier(jnp.sum(jnp.square(points.astype(jnp.float32)), axis=1))
    point_blocks = points.reshape(DEVICES, NPT, D)
    norm_blocks = norm_all.reshape(DEVICES, NPT)
    for step_index in range(STEPS):
        tile_ids = batch_tiles[step_index]
        row_ids = (jnp.arange(N_GRP, dtype=jnp.int32)[:, None, None] * GROUP_PTS + tile_ids[:, :, None] * TILE + jnp.arange(TILE, dtype=jnp.int32)[None, None, :]).reshape(-1).astype(jnp.int32)
        picked = points[row_ids]
        duals_bf = dual_weights.astype(jnp.bfloat16).reshape(DEVICES, NPT, SAMPLES)

        def add_block(running, block):
            point_block, norm_block, dual_block = block
            kernel_tile = kernel_values(picked, point_block, norm_block)
            return (running + jnp.dot(kernel_tile, dual_block, preferred_element_type=jnp.float32), None)
        summed, _ = lax.scan(add_block, jnp.zeros((BATCH, SAMPLES), jnp.float32), (point_blocks, norm_blocks, duals_bf))
        phase_arg = jnp.dot(picked, frequencies, preferred_element_type=jnp.float32) + phases[None, :]
        features = jnp.cos(phase_arg).astype(jnp.bfloat16)
        prior_vals = jnp.dot(features, prior_weights, preferred_element_type=jnp.float32) * prior_scale
        gradient = summed * inv_root + prior_vals - observed[row_ids][:, None] + noise_draws[row_ids]
        new_vel = momentum * velocity[row_ids] - step_size * gradient
        new_duals = dual_weights[row_ids] + new_vel
        dual_weights = dual_weights.at[row_ids].set(new_duals)
        velocity = velocity.at[row_ids].set(new_vel)
    return (dual_weights, velocity)
```

```python
import functools
import math

import jax
import jax.numpy as jnp
import numpy as np
from jax import lax
from jax.experimental import pallas as pl
from jax.experimental.pallas import tpu as pltpu
from jax.sharding import PartitionSpec as P

TILE = 128
CHUNK = 256

amplitude = 4.0
signal = 2.0
momentum = 0.9
step_size = 0.5

f32 = jnp.float32
bf16 = jnp.bfloat16

def cos_terms():
    degree = 6
    nodes = np.cos(np.pi * (np.arange(64) + 0.5) / 64)
    top = math.pi * math.pi * 1.0001
    squares = (nodes + 1.0) * 0.5 * top
    fit = np.polynomial.chebyshev.Chebyshev.fit(
        squares, np.cos(np.sqrt(squares)), degree, domain=[0.0, top]
    )
    return [float(c) for c in fit.convert(kind=np.polynomial.Polynomial).coef]


COS = cos_terms()
TURN_HIGH = 6.28125
TURN_LOW = 2.0 * math.pi - TURN_HIGH


def cosine(angle):
    turns = jnp.round(angle * (0.5 / math.pi))
    rest = (angle - turns * TURN_HIGH) - turns * TURN_LOW
    square = rest * rest
    total = jnp.full_like(square, COS[-1])
    for term in COS[-2::-1]:
        total = total * square + term
    return total


def rows_of(batch_ref, step, depth):
    turned = batch_ref[depth * step : depth * (step + 1), :]
    return turned, turned.astype(f32).T


def across(left, right):
    return lax.dot_general(left, right, (((1,), (1,)), ((), ())), preferred_element_type=f32)


def kernel_sum(rows, blocks, depth):
    rows_bf = rows.astype(bf16)
    row_sq = jnp.sum(rows * rows, axis=1, keepdims=True)
    total = None
    for block_ref in blocks:
        values = block_ref.shape[0] - depth
        size = block_ref.shape[1]
        step = min(size, CHUNK)
        for start in range(0, size, step):
            cut = slice(start, start + step)
            points = block_ref[values:, cut]
            wide = points.astype(f32)
            norm = jnp.sum(wide * wide, axis=0, keepdims=True)
            inner = jnp.dot(rows_bf, points, preferred_element_type=f32)
            distance = row_sq + norm - 2.0 * inner
            kern = (amplitude * jnp.exp(distance * (-1.0 / depth))).astype(bf16)
            part = across(block_ref[:values, cut], kern)
            total = part if total is None else total + part
    return total


def prior_sum(rows, freq_ref, phase_ref, weight_ref):
    rows_bf = rows.astype(bf16)
    total = None
    for start in range(0, freq_ref.shape[1], CHUNK):
        cut = slice(start, start + CHUNK)
        angle = jnp.dot(rows_bf, freq_ref[:, cut], preferred_element_type=f32) + phase_ref[0:1, cut]
        part = across(weight_ref[:, cut], cosine(angle).astype(bf16))
        total = part if total is None else total + part
    return total


def place_of(tiles_ref, step, tiles_per):
    tile = tiles_ref[step]
    mine = lax.div(tile, tiles_per) == lax.axis_index("feat")
    return mine, pl.ds(pl.multiple_of(lax.rem(tile, tiles_per) * TILE, TILE), TILE)


def data_term(tiles_ref, step, observed_ref, noise_ref):
    mine, where = place_of(tiles_ref, step, noise_ref.shape[1] // TILE)
    return mine, where, step_size * (observed_ref[0:1, where] - noise_ref[:, where])


def pack_kernel(tiles_ref, points_ref, duals_ref, batch_ref, static_ref):
    depth, count = points_ref.shape
    values = duals_ref.shape[0]
    for step in range(2):
        mine, where = place_of(tiles_ref, step, count // TILE)
        rows = points_ref[:, where]
        batch_ref[depth * step : depth * (step + 1), :] = jnp.where(mine, rows, jnp.zeros_like(rows))
    static_ref[:values, :] = duals_ref[...].astype(bf16)
    static_ref[values:, :] = points_ref[...]


def first_kernel(scales, tiles_ref, batch_ref, freq_ref, phase_ref, weight_ref, observed_ref, noise_ref, velocity_ref, *rest):
    blocks, (share_ref, send_ref) = rest[:-2], rest[-2:]
    inv_root, prior_scale = scales
    depth = freq_ref.shape[0]
    turned, rows = rows_of(batch_ref, 0, depth)
    kernel_part = kernel_sum(rows, blocks, depth)
    prior_part = prior_sum(rows, freq_ref, phase_ref, weight_ref)
    mine, where, data = data_term(tiles_ref, 0, observed_ref, noise_ref)
    base = momentum * velocity_ref[:, where] + data
    share = jnp.where(mine, base, 0.0) - step_size * (kernel_part * inv_root + prior_part * prior_scale)
    share_ref[...] = share
    send_ref[: share.shape[0], :] = share.astype(bf16)
    send_ref[share.shape[0] :, :] = turned


def second_kernel(scales, tiles_ref, batch_ref, freq_ref, phase_ref, weight_ref, observed_ref, noise_ref, *rest):
    blocks, share_ref = rest[:-1], rest[-1]
    inv_root, prior_scale = scales
    depth = freq_ref.shape[0]
    _, rows = rows_of(batch_ref, 1, depth)
    kernel_part = kernel_sum(rows, blocks, depth)
    prior_part = prior_sum(rows, freq_ref, phase_ref, weight_ref)
    mine, _, data = data_term(tiles_ref, 1, observed_ref, noise_ref)
    share_ref[...] = jnp.where(mine, data, 0.0) - step_size * (kernel_part * inv_root + prior_part * prior_scale)


def correct_kernel(scales, depth, batch_ref, first_ref, second_ref, *rest):
    blocks, total_ref = rest[:-1], rest[-1]
    _, rows = rows_of(batch_ref, 1, depth)
    moved = kernel_sum(rows, blocks, depth)
    values = first_ref.shape[0]
    total_ref[:values, :] = first_ref[...]
    total_ref[values:, :] = second_ref[...] - (step_size * scales[0]) * moved


def finish_kernel(tiles_ref, mine_ref, other_ref, duals_ref, velocity_ref, new_duals_ref, new_velocity_ref):
    values, count = duals_ref.shape
    total = mine_ref[...] + other_ref[...]
    new_duals_ref[...] = duals_ref[...]
    new_velocity_ref[...] = velocity_ref[...]
    own, where = place_of(tiles_ref, 0, count // TILE)

    @pl.when(own)
    def _():
        moved = total[:values, :]
        new_velocity_ref[:, where] = moved
        new_duals_ref[:, where] = new_duals_ref[:, where] + moved

    own_later, later = place_of(tiles_ref, 1, count // TILE)

    @pl.when(own_later)
    def _():
        moved = momentum * new_velocity_ref[:, later] + total[values:, :]
        new_velocity_ref[:, later] = moved
        new_duals_ref[:, later] = new_duals_ref[:, later] + moved


def call(kernel, outs, *args, flops=0, name=None):
    specs = [pl.BlockSpec(memory_space=pltpu.SMEM if a.dtype == jnp.int32 else pltpu.VMEM) for a in args]
    out_shape = [jax.ShapeDtypeStruct(shape, dtype) for shape, dtype in outs]
    return pl.pallas_call(
        kernel,
        out_shape=out_shape,
        in_specs=specs,
        out_specs=[pl.BlockSpec(memory_space=pltpu.VMEM)] * len(outs),
        compiler_params=pltpu.CompilerParams(vmem_limit_bytes=24 * 1024 * 1024),
        cost_estimate=pl.CostEstimate(
            flops=flops, bytes_accessed=sum(a.size * a.dtype.itemsize for a in args), transcendentals=0
        ),
        name=name,
    )(*args)


def swap(array, axis, count, bit):
    return lax.ppermute(array, axis, [(i, i ^ bit) for i in range(count)])


def over_feat(array, count):
    bit = 1
    other = None
    while bit < count:
        if other is not None:
            array = array + other
        other = swap(array, "feat", count, bit)
        bit *= 2
    return array, other


def local(points, dual_weights, velocity, observed, noise_draws, frequencies, phases, prior_weights, batch_tiles):
    groups = lax.axis_size("grp")
    members = lax.axis_size("feat")
    count, depth = points.shape
    samples = dual_weights.shape[1]
    inv_root = 1.0 / math.sqrt(count * groups * members)
    prior_scale = signal * math.sqrt(2.0 / (frequencies.shape[1] * members))
    scales = (inv_root, prior_scale)
    tiles = batch_tiles.reshape(2)
    observed = observed.reshape(1, count)
    phases = phases.reshape(1, phases.shape[0])
    points, duals, velocity, noise, weights = (a.T for a in (points, dual_weights, velocity, noise_draws, prior_weights))

    batch, static = call(
        pack_kernel, [((2 * depth, TILE), bf16), ((samples + depth, count), bf16)], tiles, points, duals, name="pack"
    )
    fixed = [static] + [swap(static, "grp", groups, k) for k in range(1, groups)]
    mine, other = over_feat(batch, members)
    batch = mine + other

    share, send = call(
        functools.partial(first_kernel, scales), [((samples, TILE), f32), ((samples + depth, TILE), bf16)],
        tiles, batch, frequencies, phases, weights, observed, noise, velocity, *fixed,
        flops=10**9, name="first",
    )
    moves = [send] + [swap(send, "grp", groups, k) for k in range(1, groups)]
    (later,) = call(
        functools.partial(second_kernel, scales), [((samples, TILE), f32)],
        tiles, batch, frequencies, phases, weights, observed, noise, *fixed,
        flops=10**9, name="second",
    )
    (total,) = call(
        functools.partial(correct_kernel, scales, depth), [((2 * samples, TILE), f32)],
        batch, share, later, *moves, flops=10**8, name="correct",
    )
    mine, other = over_feat(total, members)
    new_duals, new_velocity = call(
        finish_kernel, [((samples, count), f32)] * 2, tiles, mine, other, duals, velocity, name="finish"
    )
    return new_duals.T, new_velocity.T


def solution(mesh):
    return jax.shard_map(
        local,
        mesh=mesh,
        in_specs=(
            P(("grp", "feat"), None),
            P(("grp", "feat"), None),
            P(("grp", "feat"), None),
            P(("grp", "feat")),
            P(("grp", "feat"), None),
            P(None, "feat"),
            P("feat"),
            P("feat", None),
            P(None, "grp", None),
        ),
        out_specs=(P(("grp", "feat"), None), P(("grp", "feat"), None)),
        check_vma=False,
    )
```

```python
import functools
import math

import jax
import jax.numpy as jnp
import numpy as np
from jax import lax
from jax.experimental import pallas as pl
from jax.experimental.pallas import tpu as pltpu
from jax.sharding import PartitionSpec as P

TILE = 128
CHUNK = 256

amplitude = 4.0
signal = 2.0
momentum = 0.9
step_size = 0.5

f32 = jnp.float32
bf16 = jnp.bfloat16

SHRINK = 0.25

def cos_terms():
    nodes = np.cos(np.pi * (np.arange(64) + 0.5) / 64)
    squares = (nodes + 1.0) * 0.125
    fit = np.polynomial.chebyshev.Chebyshev.fit(
        squares, np.cos(2.0 * np.pi * np.sqrt(squares)), 6, domain=[0.0, 0.25]
    )
    return [float(c) for c in fit.convert(kind=np.polynomial.Polynomial).coef]


COS = cos_terms()
ANGLE_ROWS = 128


def cosine(turns):
    rest = turns - jnp.round(turns)
    square = rest * rest
    total = COS[-1] * square + COS[-2]
    for term in COS[-3::-1]:
        total = total * square + term
    return total


def three_parts(wide):
    high = wide.astype(bf16)
    rest = wide - high.astype(f32)
    middle = rest.astype(bf16)
    return high, middle, (rest - middle.astype(f32)).astype(bf16)


def rows_of(turned):
    wide = turned.astype(f32)
    depth, tile = wide.shape
    ids = lax.broadcasted_iota(jnp.int32, (ANGLE_ROWS - 3 * depth, tile), 0)
    upright = jnp.concatenate([wide, wide, wide, jnp.where(ids < 3, 1.0, 0.0)], axis=0).T
    return upright.astype(bf16), upright[:, :depth]


def across(left, right):
    return lax.dot_general(left, right, (((1,), (1,)), ((), ())), preferred_element_type=f32)


def kernel_sum(rows, blocks, depth):
    rows_bf = rows.astype(bf16)
    scale = -math.log2(math.e) / depth
    row_part = jnp.sum(rows * rows, axis=1, keepdims=True) * scale + math.log2(amplitude)
    total = None
    for block_ref in blocks:
        values = block_ref.shape[0] - depth
        size = block_ref.shape[1]
        step = min(size, CHUNK)
        for start in range(0, size, step):
            cut = slice(start, start + step)
            points = block_ref[values:, cut]
            wide = points.astype(f32)
            norm_part = jnp.sum(wide * wide, axis=0, keepdims=True) * scale
            inner = jnp.dot(rows_bf, points, preferred_element_type=f32)
            kern = jnp.exp2(inner * (-2.0 * scale) + (row_part + norm_part)).astype(bf16)
            part = across(block_ref[:values, cut], kern)
            total = part if total is None else total + part
    return total


def prior_sum(upright, angle_ref, weight_ref):
    total = None
    for start in range(0, angle_ref.shape[1], CHUNK):
        cut = slice(start, start + CHUNK)
        turns = jnp.dot(upright, angle_ref[:, cut], preferred_element_type=f32)
        part = across(weight_ref[:, cut], cosine(turns).astype(bf16))
        total = part if total is None else total + part
    return total


def place_of(tiles_ref, step, tiles_per):
    tile = tiles_ref[step]
    mine = lax.div(tile, tiles_per) == lax.axis_index("feat")
    return mine, pl.ds(pl.multiple_of(lax.rem(tile, tiles_per) * TILE, TILE), TILE)


def fetch(pairs, sems):
    copies = [pltpu.make_async_copy(src, dst, sems.at[k]) for k, (src, dst) in enumerate(pairs)]
    for copy in copies:
        copy.start()
    for copy in copies:
        copy.wait()


def pack_kernel(tiles_hbm, points_hbm, duals_hbm, batch_ref, static_ref, tiles_ref, points_ref, duals_ref, sems):
    fetch([(tiles_hbm, tiles_ref), (points_hbm, points_ref), (duals_hbm, duals_ref)], sems)
    depth, count = points_ref.shape
    values = duals_ref.shape[0]
    for step in range(2):
        mine, where = place_of(tiles_ref, step, count // TILE)
        rows = points_ref[:, where]
        batch_ref[depth * step : depth * (step + 1), :] = jnp.where(mine, rows, jnp.zeros_like(rows))
    static_ref[:values, :] = duals_ref[...].astype(bf16)
    static_ref[values:, :] = points_ref[...]


def prepare_kernel(
    tiles_hbm, freq_hbm, phase_hbm, weight_hbm, observed_hbm, noise_hbm, velocity_hbm, duals_hbm,
    angle_ref, weight_ref, base_ref, later_ref, marks_ref, velocity_ref, duals_ref,
    tiles_ref, freq_ref, phase_ref, observed_ref, noise_ref, sems,
):
    fetch(
        [
            (freq_hbm, freq_ref), (phase_hbm, phase_ref), (weight_hbm, weight_ref), (tiles_hbm, tiles_ref),
            (observed_hbm, observed_ref), (noise_hbm, noise_ref), (velocity_hbm, velocity_ref), (duals_hbm, duals_ref),
        ],
        sems,
    )
    depth, count = freq_ref.shape
    a_turn = 0.5 / math.pi
    for k, part in enumerate(three_parts(freq_ref[...].astype(f32) * a_turn)):
        angle_ref[depth * k : depth * (k + 1), :] = part
    pad = ANGLE_ROWS - 3 * depth
    ids = lax.broadcasted_iota(jnp.int32, (pad, count), 0)
    tail = jnp.zeros((pad, count), f32)
    for k, part in enumerate(three_parts(phase_ref[...] * a_turn)):
        tail = jnp.where(ids == k, part.astype(f32), tail)
    angle_ref[3 * depth :, :] = tail.astype(bf16)

    count = velocity_ref.shape[1]
    columns = lax.broadcasted_iota(jnp.int32, (8, count), 1)
    for step, share_ref in enumerate((base_ref, later_ref)):
        mine, where = place_of(tiles_ref, step, count // TILE)
        share = step_size * (observed_ref[0:1, where] - noise_ref[:, where])
        if step == 0:
            share = share + momentum * velocity_ref[:, where]
        share_ref[...] = jnp.where(mine, share, 0.0)
        inside = (columns >= where.start) & (columns < where.start + TILE)
        marks_ref[8 * step : 8 * (step + 1), :] = jnp.where(mine & inside, 1.0, 0.0)


def share_of(scales, upright, rows, angle_ref, weight_ref, base_ref, blocks):
    inv_root, prior_scale = scales
    kernel_part = kernel_sum(rows, blocks, rows.shape[1])
    prior_part = prior_sum(upright, angle_ref, weight_ref)
    return base_ref[...] - (step_size * inv_root) * kernel_part - (step_size * prior_scale) * prior_part


def first_kernel(scales, parts, angle_ref, weight_ref, base_ref, *rest):
    terms, blocks, (share_ref, send_ref, batch_ref) = rest[:parts], rest[parts:-3], rest[-3:]
    batch = terms[0][...]
    for term_ref in terms[1:]:
        batch = batch + term_ref[...]
    batch_ref[...] = batch
    depth = batch.shape[0] // 2
    upright, rows = rows_of(batch[:depth])
    share = share_of(scales, upright, rows, angle_ref, weight_ref, base_ref, blocks)
    share_ref[...] = share
    send_ref[: share.shape[0], :] = share.astype(bf16)
    send_ref[share.shape[0] :, :] = batch[:depth]


def second_kernel(scales, angle_ref, weight_ref, later_ref, batch_ref, *rest):
    blocks, share_ref = rest[:-1], rest[-1]
    upright, rows = rows_of(batch_ref[batch_ref.shape[0] // 2 :, :])
    share_ref[...] = share_of(scales, upright, rows, angle_ref, weight_ref, later_ref, blocks)


def correct_kernel(scales, batch_ref, first_ref, second_ref, *rest):
    blocks, total_ref = rest[:-1], rest[-1]
    _, rows = rows_of(batch_ref[batch_ref.shape[0] // 2 :, :])
    moved = kernel_sum(rows, blocks, rows.shape[1])
    values = first_ref.shape[0]
    total_ref[:values, :] = first_ref[...]
    total_ref[values:, :] = second_ref[...] - (step_size * scales[0]) * moved


def finish_kernel(marks_ref, total_ref, duals_ref, velocity_ref, new_duals_ref, new_velocity_ref):
    values, count = duals_ref.shape
    repeats = count // TILE
    total = jnp.concatenate([total_ref[...]] * repeats, axis=1)
    first, second = marks_ref[0:1, :] > 0.0, marks_ref[8:9, :] > 0.0
    velocity, duals = velocity_ref[...], duals_ref[...]
    moved = total[:values, :]
    velocity = jnp.where(first, moved, velocity)
    duals = jnp.where(first, duals + moved, duals)
    moved = momentum * velocity + total[values:, :]
    new_velocity_ref[...] = jnp.where(second, moved, velocity)
    new_duals_ref[...] = jnp.where(second, duals + moved, duals)


def call(kernel, outs, *args, flops=0, name=None, from_hbm=False):
    small, large = pltpu.SMEM, pltpu.VMEM
    scratch = []
    if from_hbm:
        small = large = pltpu.HBM
        args = [pltpu.with_memory_space_constraint(a, pltpu.HBM) for a in args]
        scratch = [
            (pltpu.SMEM if a.dtype == jnp.int32 else pltpu.VMEM)(a.shape, a.dtype) for k, a in enumerate(args) if k not in from_hbm
        ] + [pltpu.SemaphoreType.DMA((len(args),))]
    return pl.pallas_call(
        kernel,
        out_shape=[jax.ShapeDtypeStruct(shape, dtype) for shape, dtype in outs],
        in_specs=[pl.BlockSpec(memory_space=small if a.dtype == jnp.int32 else large) for a in args],
        out_specs=[pl.BlockSpec(memory_space=pltpu.VMEM)] * len(outs),
        scratch_shapes=scratch,
        compiler_params=pltpu.CompilerParams(vmem_limit_bytes=24 * 1024 * 1024),
        cost_estimate=pl.CostEstimate(
            flops=flops, bytes_accessed=sum(a.size * a.dtype.itemsize for a in args), transcendentals=0
        ),
        name=name,
    )(*args)


def swap(array, groups, members, group_bits, member_bits):
    pairs = [
        (g * members + m, (g ^ group_bits) * members + (m ^ member_bits)) for g in range(groups) for m in range(members)
    ]
    return lax.ppermute(array, ("grp", "feat"), pairs)


def local(points, dual_weights, velocity, observed, noise_draws, frequencies, phases, prior_weights, batch_tiles):
    groups = lax.axis_size("grp")
    members = lax.axis_size("feat")
    count, depth = points.shape
    samples = dual_weights.shape[1]
    features = frequencies.shape[1]
    scales = (1.0 / math.sqrt(count * groups * members), signal * math.sqrt(2.0 / (features * members)))
    tiles = batch_tiles.reshape(2)
    observed = observed.reshape(1, count)
    phases = phases.reshape(1, features)
    points, duals, velocity, noise, weights = (a.T for a in (points, dual_weights, velocity, noise_draws, prior_weights))
    part = (samples, TILE)

    def other_core(array):
        return swap(array, groups, members, 0, 1)

    def other_chips(array):
        return [swap(array, groups, members, 0, 2 * k + 1) for k in range(1, members // 2)]

    def other_groups(array):
        return [swap(array, groups, members, k, 1) for k in range(1, groups)]

    batch, static = call(
        pack_kernel, [((2 * depth, TILE), bf16), ((samples + depth, count), bf16)], tiles, points, duals,
        name="pack", from_hbm=(-1,),
    )
    fixed = [static] + other_groups(static)
    batch = batch + other_core(batch)
    batch = [batch] + other_chips(batch)
    whole = (samples, count)
    angles, weights, base, later, marks, velocity, duals = call(
        prepare_kernel,
        [((ANGLE_ROWS, features), bf16), ((samples, features), bf16), (part, f32), (part, f32),
         ((16, count), f32), (whole, f32), (whole, f32)],
        tiles, frequencies, phases, weights, observed, noise, velocity, duals,
        name="prepare", from_hbm=(3, 6, 7), flops=10**8,
    )
    share, send, batch = call(
        functools.partial(first_kernel, scales, len(batch)),
        [(part, f32), ((samples + depth, TILE), bf16), ((2 * depth, TILE), bf16)],
        angles, weights, base, *batch, *fixed,
        flops=10**9, name="first",
    )
    moves = [send] + other_groups(send)
    (later,) = call(
        functools.partial(second_kernel, scales), [(part, f32)], angles, weights, later, batch, *fixed,
        flops=10**9, name="second",
    )
    (total,) = call(
        functools.partial(correct_kernel, scales), [((2 * samples, TILE), f32)],
        batch, share, later, *moves, flops=10**8, name="correct",
    )
    total = total + other_core(total)
    for term in other_chips((total * SHRINK).astype(jnp.float16)):
        total = total + term.astype(f32) * (1.0 / SHRINK)
    new_duals, new_velocity = call(
        finish_kernel, [(whole, f32)] * 2, marks, total, duals, velocity, name="finish"
    )
    return new_duals.T, new_velocity.T


def solution(mesh):
    return jax.shard_map(
        local,
        mesh=mesh,
        in_specs=(
            P(("grp", "feat"), None),
            P(("grp", "feat"), None),
            P(("grp", "feat"), None),
            P(("grp", "feat")),
            P(("grp", "feat"), None),
            P(None, "feat"),
            P("feat"),
            P("feat", None),
            P(None, "grp", None),
        ),
        out_specs=(P(("grp", "feat"), None), P(("grp", "feat"), None)),
        check_vma=False,
    )
```

```python
import functools
import math

import jax
import jax.numpy as jnp
import numpy as np
from jax import lax
from jax.experimental import pallas as pl
from jax.experimental.pallas import tpu as pltpu
from jax.sharding import PartitionSpec as P

TILE = 128
CHUNK = 256

amplitude = 4.0
signal = 2.0
momentum = 0.9
step_size = 0.5

f32 = jnp.float32
bf16 = jnp.bfloat16

SHRINK = 0.25

def cos_terms():
    nodes = np.cos(np.pi * (np.arange(64) + 0.5) / 64)
    squares = (nodes + 1.0) * 0.125
    fit = np.polynomial.chebyshev.Chebyshev.fit(
        squares, np.cos(2.0 * np.pi * np.sqrt(squares)), 5, domain=[0.0, 0.25]
    )
    return [float(c) for c in fit.convert(kind=np.polynomial.Polynomial).coef]


COS = cos_terms()
ANGLE_ROWS = 128


def cosine(turns):
    rest = turns - jnp.round(turns)
    square = rest * rest
    total = COS[-1] * square + COS[-2]
    for term in COS[-3::-1]:
        total = total * square + term
    return total


def three_parts(wide):
    high = wide.astype(bf16)
    rest = wide - high.astype(f32)
    middle = rest.astype(bf16)
    return high, middle, (rest - middle.astype(f32)).astype(bf16)


def rows_of(turned):
    wide = turned.astype(f32)
    depth, tile = wide.shape
    ids = lax.broadcasted_iota(jnp.int32, (ANGLE_ROWS - 3 * depth, tile), 0)
    upright = jnp.concatenate([wide, wide, wide, jnp.where(ids < 3, 1.0, 0.0)], axis=0).T
    return upright.astype(bf16), upright[:, :depth]


def across(left, right):
    return lax.dot_general(left, right, (((1,), (1,)), ((), ())), preferred_element_type=f32)


def kernel_sum(rows, blocks, depth):
    rows_bf = rows.astype(bf16)
    scale = -math.log2(math.e) / depth
    row_part = jnp.sum(rows * rows, axis=1, keepdims=True) * scale + math.log2(amplitude)
    total = None
    for block_ref in blocks:
        values = block_ref.shape[0] - depth
        size = block_ref.shape[1]
        step = min(size, CHUNK)
        for start in range(0, size, step):
            cut = slice(start, start + step)
            points = block_ref[values:, cut]
            wide = points.astype(f32)
            norm_part = jnp.sum(wide * wide, axis=0, keepdims=True) * scale
            inner = jnp.dot(rows_bf, points, preferred_element_type=f32)
            kern = jnp.exp2(inner * (-2.0 * scale) + (row_part + norm_part)).astype(bf16)
            part = across(block_ref[:values, cut], kern)
            total = part if total is None else total + part
    return total


def prior_sum(upright, angle_ref, weight_ref):
    total = None
    for start in range(0, angle_ref.shape[1], CHUNK):
        cut = slice(start, start + CHUNK)
        turns = jnp.dot(upright, angle_ref[:, cut], preferred_element_type=f32)
        part = across(weight_ref[:, cut], cosine(turns).astype(bf16))
        total = part if total is None else total + part
    return total


def place_of(tiles_ref, step, tiles_per, core=0):
    tile = tiles_ref[step]
    mine = lax.div(tile, tiles_per) == lax.bitwise_xor(lax.axis_index("feat"), core)
    return mine, pl.ds(pl.multiple_of(lax.rem(tile, tiles_per) * TILE, TILE), TILE)


def fetch(pairs, sems):
    copies = [pltpu.make_async_copy(src, dst, sems.at[k]) for k, (src, dst) in enumerate(pairs)]
    for copy in copies:
        copy.start()
    for copy in copies:
        copy.wait()


def pack_kernel(marks_ref, points_ref, other_ref, duals_ref, batch_ref, static_ref):
    depth, count = points_ref.shape
    values = duals_ref.shape[0]
    for step in range(2):
        rows = None
        for core, from_ref in enumerate((points_ref, other_ref)):
            row = 8 * (step + 2 * core)
            kept = jnp.where(marks_ref[row : row + 1, :] > 0.0, from_ref[...].astype(f32), 0.0)
            for start in range(0, count, TILE):
                piece = kept[:, start : start + TILE]
                rows = piece if rows is None else rows + piece
        batch_ref[depth * step : depth * (step + 1), :] = rows.astype(bf16)
    static_ref[:values, :] = duals_ref[...].astype(bf16)
    static_ref[values:, :] = points_ref[...]


def prepare_kernel(
    tiles_hbm, freq_hbm, phase_hbm, weight_hbm, observed_hbm, noise_hbm, velocity_hbm, duals_hbm, points_hbm,
    angle_ref, weight_ref, base_ref, later_ref, marks_ref, velocity_ref, duals_ref, points_ref,
    tiles_ref, freq_ref, phase_ref, observed_ref, noise_ref, sems,
):
    fetch(
        [
            (freq_hbm, freq_ref), (phase_hbm, phase_ref), (weight_hbm, weight_ref), (tiles_hbm, tiles_ref),
            (observed_hbm, observed_ref), (noise_hbm, noise_ref), (velocity_hbm, velocity_ref), (duals_hbm, duals_ref),
            (points_hbm, points_ref),
        ],
        sems,
    )
    depth, count = freq_ref.shape
    a_turn = 0.5 / math.pi
    for k, part in enumerate(three_parts(freq_ref[...].astype(f32) * a_turn)):
        angle_ref[depth * k : depth * (k + 1), :] = part
    pad = ANGLE_ROWS - 3 * depth
    ids = lax.broadcasted_iota(jnp.int32, (pad, count), 0)
    tail = jnp.zeros((pad, count), f32)
    for k, part in enumerate(three_parts(phase_ref[...] * a_turn)):
        tail = jnp.where(ids == k, part.astype(f32), tail)
    angle_ref[3 * depth :, :] = tail.astype(bf16)

    count = velocity_ref.shape[1]
    columns = lax.broadcasted_iota(jnp.int32, (8, count), 1)
    for step, share_ref in enumerate((base_ref, later_ref)):
        mine, where = place_of(tiles_ref, step, count // TILE)
        share = step_size * (observed_ref[0:1, where] - noise_ref[:, where])
        if step == 0:
            share = share + momentum * velocity_ref[:, where]
        share_ref[...] = jnp.where(mine, share, 0.0)
        inside = (columns >= where.start) & (columns < where.start + TILE)
        marks_ref[8 * step : 8 * (step + 1), :] = jnp.where(mine & inside, 1.0, 0.0)
        mine, _ = place_of(tiles_ref, step, count // TILE, 1)
        marks_ref[8 * (step + 2) : 8 * (step + 3), :] = jnp.where(mine & inside, 1.0, 0.0)


def share_of(scales, upright, rows, angle_ref, weight_ref, base_ref, blocks):
    inv_root, prior_scale = scales
    kernel_part = kernel_sum(rows, blocks, rows.shape[1])
    prior_part = prior_sum(upright, angle_ref, weight_ref)
    return base_ref[...] - (step_size * inv_root) * kernel_part - (step_size * prior_scale) * prior_part


def first_kernel(scales, parts, angle_ref, weight_ref, base_ref, *rest):
    terms, blocks, (share_ref, send_ref, batch_ref) = rest[:parts], rest[parts:-3], rest[-3:]
    batch = terms[0][...]
    for term_ref in terms[1:]:
        batch = batch + term_ref[...]
    batch_ref[...] = batch
    depth = batch.shape[0] // 2
    upright, rows = rows_of(batch[:depth])
    share = share_of(scales, upright, rows, angle_ref, weight_ref, base_ref, blocks)
    share_ref[...] = share
    send_ref[: share.shape[0], :] = share.astype(bf16)
    send_ref[share.shape[0] :, :] = batch[:depth]


def second_kernel(scales, angle_ref, weight_ref, later_ref, batch_ref, *rest):
    blocks, share_ref = rest[:-1], rest[-1]
    upright, rows = rows_of(batch_ref[batch_ref.shape[0] // 2 :, :])
    share_ref[...] = share_of(scales, upright, rows, angle_ref, weight_ref, later_ref, blocks)


def correct_kernel(scales, batch_ref, first_ref, second_ref, *rest):
    blocks, total_ref = rest[:-1], rest[-1]
    _, rows = rows_of(batch_ref[batch_ref.shape[0] // 2 :, :])
    moved = kernel_sum(rows, blocks, rows.shape[1])
    values = first_ref.shape[0]
    total_ref[:values, :] = first_ref[...]
    total_ref[values:, :] = second_ref[...] - (step_size * scales[0]) * moved


def finish_kernel(marks_ref, total_ref, duals_ref, velocity_ref, new_duals_ref, new_velocity_ref):
    values, count = duals_ref.shape
    repeats = count // TILE
    total = jnp.concatenate([total_ref[...]] * repeats, axis=1)
    first, second = marks_ref[0:1, :] > 0.0, marks_ref[8:9, :] > 0.0
    velocity, duals = velocity_ref[...], duals_ref[...]
    moved = total[:values, :]
    velocity = jnp.where(first, moved, velocity)
    duals = jnp.where(first, duals + moved, duals)
    moved = momentum * velocity + total[values:, :]
    new_velocity_ref[...] = jnp.where(second, moved, velocity)
    new_duals_ref[...] = jnp.where(second, duals + moved, duals)


def call(kernel, outs, *args, flops=0, name=None, from_hbm=False):
    small, large = pltpu.SMEM, pltpu.VMEM
    scratch = []
    if from_hbm:
        small = large = pltpu.HBM
        args = [pltpu.with_memory_space_constraint(a, pltpu.HBM) for a in args]
        scratch = [
            (pltpu.SMEM if a.dtype == jnp.int32 else pltpu.VMEM)(a.shape, a.dtype) for k, a in enumerate(args) if k not in from_hbm
        ] + [pltpu.SemaphoreType.DMA((len(args),))]
    return pl.pallas_call(
        kernel,
        out_shape=[jax.ShapeDtypeStruct(shape, dtype) for shape, dtype in outs],
        in_specs=[pl.BlockSpec(memory_space=small if a.dtype == jnp.int32 else large) for a in args],
        out_specs=[pl.BlockSpec(memory_space=pltpu.VMEM)] * len(outs),
        scratch_shapes=scratch,
        compiler_params=pltpu.CompilerParams(vmem_limit_bytes=24 * 1024 * 1024),
        cost_estimate=pl.CostEstimate(
            flops=flops, bytes_accessed=sum(a.size * a.dtype.itemsize for a in args), transcendentals=0
        ),
        name=name,
    )(*args)


def swap(array, groups, members, group_bits, member_bits):
    pairs = [
        (g * members + m, (g ^ group_bits) * members + (m ^ member_bits)) for g in range(groups) for m in range(members)
    ]
    return lax.ppermute(array, ("grp", "feat"), pairs)


def local(points, dual_weights, velocity, observed, noise_draws, frequencies, phases, prior_weights, batch_tiles):
    groups = lax.axis_size("grp")
    members = lax.axis_size("feat")
    count, depth = points.shape
    samples = dual_weights.shape[1]
    features = frequencies.shape[1]
    scales = (1.0 / math.sqrt(count * groups * members), signal * math.sqrt(2.0 / (features * members)))
    tiles = batch_tiles.reshape(2)
    observed = observed.reshape(1, count)
    phases = phases.reshape(1, features)
    points, duals, velocity, noise, weights = (a.T for a in (points, dual_weights, velocity, noise_draws, prior_weights))
    part = (samples, TILE)

    def other_core(array):
        return swap(array, groups, members, 0, 1)

    def other_chips(array):
        return [swap(array, groups, members, 0, 2 * k + 1) for k in range(1, members // 2)]

    def other_groups(array):
        return [swap(array, groups, members, k, 1) for k in range(1, groups)]

    whole = (samples, count)
    other_points = other_core(points)
    angles, weights, base, later, marks, velocity, duals, points = call(
        prepare_kernel,
        [((ANGLE_ROWS, features), bf16), ((samples, features), bf16), (part, f32), (part, f32),
         ((32, count), f32), (whole, f32), (whole, f32), ((depth, count), bf16)],
        tiles, frequencies, phases, weights, observed, noise, velocity, duals, points,
        name="prepare", from_hbm=(3, 6, 7, 8), flops=10**8,
    )
    batch, static = call(
        pack_kernel, [((2 * depth, TILE), bf16), ((samples + depth, count), bf16)], marks, points, other_points, duals,
        name="pack",
    )
    batch, fixed = [batch], [static]
    chip_bit, group_bit = 2, 1
    while chip_bit < members or group_bit < groups:
        if group_bit < groups:
            wide = jnp.concatenate(fixed, axis=1) if len(fixed) > 1 else static
            fixed.append(swap(wide, groups, members, group_bit, 1))
        if chip_bit < members:
            whole_batch = sum(batch[1:], batch[0])
            batch = [whole_batch, swap(whole_batch, groups, members, 0, chip_bit + 1)]
        if 2 * group_bit < groups and 2 * chip_bit < members:
            fixed[-1], batch[1] = lax.optimization_barrier((fixed[-1], batch[1]))
        chip_bit, group_bit = 2 * chip_bit, 2 * group_bit

    share, send, batch = call(
        functools.partial(first_kernel, scales, len(batch)),
        [(part, f32), ((samples + depth, TILE), bf16), ((2 * depth, TILE), bf16)],
        angles, weights, base, *batch, *fixed,
        flops=10**9, name="first",
    )
    moves = [send] + other_groups(send)
    (later,) = call(
        functools.partial(second_kernel, scales), [(part, f32)], angles, weights, later, batch, *fixed,
        flops=10**9, name="second",
    )
    (total,) = call(
        functools.partial(correct_kernel, scales), [((2 * samples, TILE), f32)],
        batch, share, later, *moves, flops=10**8, name="correct",
    )
    total = total + other_core(total)
    bit = 2
    while bit < members:
        total = total + swap((total * SHRINK).astype(jnp.float16), groups, members, 0, bit + 1).astype(f32) * (1.0 / SHRINK)
        bit *= 2
    new_duals, new_velocity = call(
        finish_kernel, [(whole, f32)] * 2, marks, total, duals, velocity, name="finish"
    )
    return new_duals.T, new_velocity.T


def solution(mesh):
    return jax.shard_map(
        local,
        mesh=mesh,
        in_specs=(
            P(("grp", "feat"), None),
            P(("grp", "feat"), None),
            P(("grp", "feat"), None),
            P(("grp", "feat")),
            P(("grp", "feat"), None),
            P(None, "feat"),
            P("feat"),
            P("feat", None),
            P(None, "grp", None),
        ),
        out_specs=(P(("grp", "feat"), None), P(("grp", "feat"), None)),
        check_vma=False,
    )
```

```python
import functools
import math

import jax
import jax.numpy as jnp
import numpy as np
from jax import lax
from jax.experimental import pallas as pl
from jax.experimental.pallas import tpu as pltpu
from jax.sharding import PartitionSpec as P

TILE = 128
CHUNK = 256

amplitude = 4.0
signal = 2.0
momentum = 0.9
step_size = 0.5

f32 = jnp.float32
bf16 = jnp.bfloat16

SHRINK = 0.25

def cos_terms():
    nodes = np.cos(np.pi * (np.arange(64) + 0.5) / 64)
    squares = (nodes + 1.0) * 0.125
    fit = np.polynomial.chebyshev.Chebyshev.fit(
        squares, np.cos(2.0 * np.pi * np.sqrt(squares)), 5, domain=[0.0, 0.25]
    )
    return [float(c) for c in fit.convert(kind=np.polynomial.Polynomial).coef]


COS = cos_terms()
ANGLE_ROWS = 128


def cosine(turns):
    rest = turns - jnp.round(turns)
    square = rest * rest
    total = COS[-1] * square + COS[-2]
    for term in COS[-3::-1]:
        total = total * square + term
    return total


def three_parts(wide):
    high = wide.astype(bf16)
    rest = wide - high.astype(f32)
    middle = rest.astype(bf16)
    return high, middle, (rest - middle.astype(f32)).astype(bf16)


def rows_of(turned):
    wide = turned.astype(f32)
    depth, tile = wide.shape
    ids = lax.broadcasted_iota(jnp.int32, (ANGLE_ROWS - 3 * depth, tile), 0)
    upright = jnp.concatenate([wide, wide, wide, jnp.where(ids < 3, 1.0, 0.0)], axis=0).T
    return upright.astype(bf16), upright[:, :depth]


def across(left, right):
    return lax.dot_general(left, right, (((1,), (1,)), ((), ())), preferred_element_type=f32)


def kernel_sum(rows, blocks, depth):
    rows_bf = rows.astype(bf16)
    scale = -math.log2(math.e) / depth
    row_part = jnp.sum(rows * rows, axis=1, keepdims=True) * scale + math.log2(amplitude)
    total = None
    for block_ref in blocks:
        values = block_ref.shape[0] - depth
        size = block_ref.shape[1]
        step = min(size, CHUNK)
        for start in range(0, size, step):
            cut = slice(start, start + step)
            points = block_ref[values:, cut]
            wide = points.astype(f32)
            norm_part = jnp.sum(wide * wide, axis=0, keepdims=True) * scale
            inner = jnp.dot(rows_bf, points, preferred_element_type=f32)
            kern = jnp.exp2(inner * (-2.0 * scale) + (row_part + norm_part)).astype(bf16)
            part = across(block_ref[:values, cut], kern)
            total = part if total is None else total + part
    return total


def prior_sum(upright, angle_ref, weight_ref):
    total = None
    for start in range(0, angle_ref.shape[1], CHUNK):
        cut = slice(start, start + CHUNK)
        turns = jnp.dot(upright, angle_ref[:, cut], preferred_element_type=f32)
        part = across(weight_ref[:, cut], cosine(turns).astype(bf16))
        total = part if total is None else total + part
    return total


PLACE, PACK, PREPARE = 2 * 10**9, 10**9, 10**9


def place_of(tiles_ref, step, tiles_per, core=0):
    tile = tiles_ref[step]
    mine = lax.div(tile, tiles_per) == lax.bitwise_xor(lax.axis_index("feat"), core)
    return mine, pl.ds(pl.multiple_of(lax.rem(tile, tiles_per) * TILE, TILE), TILE)


def fetch(pairs, sems):
    copies = [pltpu.make_async_copy(src, dst, sems.at[k]) for k, (src, dst) in enumerate(pairs)]
    for copy in copies:
        copy.start()
    for copy in copies:
        copy.wait()


def place_kernel(tiles_hbm, points_hbm, duals_hbm, marks_ref, static_ref, tiles_ref, points_ref, duals_ref, sems):
    fetch([(tiles_hbm, tiles_ref), (points_hbm, points_ref), (duals_hbm, duals_ref)], sems)
    count = points_ref.shape[1]
    values = duals_ref.shape[0]
    columns = lax.broadcasted_iota(jnp.int32, (8, count), 1)
    for core in range(2):
        for step in range(2):
            mine, where = place_of(tiles_ref, step, count // TILE, core)
            inside = (columns >= where.start) & (columns < where.start + TILE)
            row = 8 * (step + 2 * core)
            marks_ref[row : row + 8, :] = jnp.where(mine & inside, 1.0, 0.0)
    static_ref[:values, :] = duals_ref[...].astype(bf16)
    static_ref[values:, :] = points_ref[...]


def pack_kernel(marks_ref, static_ref, other_ref, batch_ref):
    depth, count = other_ref.shape
    values = static_ref.shape[0] - depth
    for step in range(2):
        rows = None
        for core, points in enumerate((static_ref[values:, :], other_ref[...])):
            row = 8 * (step + 2 * core)
            kept = jnp.where(marks_ref[row : row + 1, :] > 0.0, points.astype(f32), 0.0)
            for start in range(0, count, TILE):
                piece = kept[:, start : start + TILE]
                rows = piece if rows is None else rows + piece
        batch_ref[depth * step : depth * (step + 1), :] = rows.astype(bf16)


def prepare_kernel(
    freq_hbm, phase_hbm, weight_hbm, observed_hbm, noise_hbm, velocity_hbm, duals_hbm, marks_ref,
    angle_ref, weight_ref, base_ref, velocity_ref, duals_ref,
    freq_ref, phase_ref, observed_ref, noise_ref, sems,
):
    fetch(
        [
            (freq_hbm, freq_ref), (phase_hbm, phase_ref), (weight_hbm, weight_ref),
            (observed_hbm, observed_ref), (noise_hbm, noise_ref), (velocity_hbm, velocity_ref), (duals_hbm, duals_ref),
        ],
        sems,
    )
    depth, count = freq_ref.shape
    a_turn = 0.5 / math.pi
    for k, part in enumerate(three_parts(freq_ref[...].astype(f32) * a_turn)):
        angle_ref[depth * k : depth * (k + 1), :] = part
    pad = ANGLE_ROWS - 3 * depth
    ids = lax.broadcasted_iota(jnp.int32, (pad, count), 0)
    tail = jnp.zeros((pad, count), f32)
    for k, part in enumerate(three_parts(phase_ref[...] * a_turn)):
        tail = jnp.where(ids == k, part.astype(f32), tail)
    angle_ref[3 * depth :, :] = tail.astype(bf16)

    values, count = velocity_ref.shape
    data = step_size * (observed_ref[...] - noise_ref[...])
    for step in range(2):
        here = data + momentum * velocity_ref[...] if step == 0 else data
        here = jnp.where(marks_ref[8 * step : 8 * step + 1, :] > 0.0, here, 0.0)
        share = here[:, :TILE]
        for start in range(TILE, count, TILE):
            share = share + here[:, start : start + TILE]
        base_ref[values * step : values * (step + 1), :] = share


def stand_kernel(*refs):
    terms, (batch_ref, upright_ref, rows_ref) = refs[:-3], refs[-3:]
    batch = terms[0][...]
    for term_ref in terms[1:]:
        batch = batch + term_ref[...]
    batch_ref[...] = batch
    depth = batch.shape[0] // 2
    for step in range(2):
        upright, rows = rows_of(batch[depth * step : depth * (step + 1)])
        upright_ref[TILE * step : TILE * (step + 1), :] = upright
        rows_ref[TILE * step : TILE * (step + 1), :] = rows


def share_of(scales, step, upright_ref, rows_ref, angle_ref, weight_ref, base_ref, blocks):
    inv_root, prior_scale = scales
    cut = slice(TILE * step, TILE * (step + 1))
    rows = rows_ref[cut, :]
    kernel_part = kernel_sum(rows, blocks, rows.shape[1])
    prior_part = prior_sum(upright_ref[cut, :], angle_ref, weight_ref)
    values = prior_part.shape[0]
    base = base_ref[values * step : values * (step + 1), :]
    return base - (step_size * inv_root) * kernel_part - (step_size * prior_scale) * prior_part


def first_kernel(scales, angle_ref, weight_ref, base_ref, batch_ref, upright_ref, rows_ref, *rest):
    blocks, (share_ref, send_ref) = rest[:-2], rest[-2:]
    share = share_of(scales, 0, upright_ref, rows_ref, angle_ref, weight_ref, base_ref, blocks)
    share_ref[...] = share
    send_ref[: share.shape[0], :] = share.astype(bf16)
    send_ref[share.shape[0] :, :] = batch_ref[: batch_ref.shape[0] // 2, :]


def second_kernel(scales, angle_ref, weight_ref, base_ref, upright_ref, rows_ref, *rest):
    blocks, share_ref = rest[:-1], rest[-1]
    share_ref[...] = share_of(scales, 1, upright_ref, rows_ref, angle_ref, weight_ref, base_ref, blocks)


def correct_kernel(scales, rows_ref, first_ref, second_ref, *rest):
    blocks, total_ref = rest[:-1], rest[-1]
    rows = rows_ref[TILE:, :]
    moved = kernel_sum(rows, blocks, rows.shape[1])
    values = first_ref.shape[0]
    total_ref[:values, :] = first_ref[...]
    total_ref[values:, :] = second_ref[...] - (step_size * scales[0]) * moved


def finish_kernel(marks_ref, total_ref, duals_ref, velocity_ref, new_duals_ref, new_velocity_ref):
    values, count = duals_ref.shape
    repeats = count // TILE
    total = jnp.concatenate([total_ref[...]] * repeats, axis=1)
    first, second = marks_ref[0:1, :] > 0.0, marks_ref[8:9, :] > 0.0
    velocity, duals = velocity_ref[...], duals_ref[...]
    moved = total[:values, :]
    velocity = jnp.where(first, moved, velocity)
    duals = jnp.where(first, duals + moved, duals)
    moved = momentum * velocity + total[values:, :]
    new_velocity_ref[...] = jnp.where(second, moved, velocity)
    new_duals_ref[...] = jnp.where(second, duals + moved, duals)


def call(kernel, outs, *args, flops=0, name=None, from_hbm=(), scratch_for=()):
    args = [pltpu.with_memory_space_constraint(a, pltpu.HBM) if k in from_hbm else a for k, a in enumerate(args)]
    scratch = [(pltpu.SMEM if args[k].dtype == jnp.int32 else pltpu.VMEM)(args[k].shape, args[k].dtype) for k in scratch_for]
    if from_hbm:
        scratch.append(pltpu.SemaphoreType.DMA((len(from_hbm),)))
    return pl.pallas_call(
        kernel,
        out_shape=[jax.ShapeDtypeStruct(shape, dtype) for shape, dtype in outs],
        in_specs=[pl.BlockSpec(memory_space=pltpu.HBM if k in from_hbm else pltpu.VMEM) for k in range(len(args))],
        out_specs=[pl.BlockSpec(memory_space=pltpu.VMEM)] * len(outs),
        scratch_shapes=scratch,
        compiler_params=pltpu.CompilerParams(vmem_limit_bytes=24 * 1024 * 1024),
        cost_estimate=pl.CostEstimate(
            flops=flops, bytes_accessed=sum(a.size * a.dtype.itemsize for a in args), transcendentals=0
        ),
        name=name,
    )(*args)


def swap(array, groups, members, group_bits, member_bits):
    pairs = [
        (g * members + m, (g ^ group_bits) * members + (m ^ member_bits)) for g in range(groups) for m in range(members)
    ]
    return lax.ppermute(array, ("grp", "feat"), pairs)


def local(points, dual_weights, velocity, observed, noise_draws, frequencies, phases, prior_weights, batch_tiles):
    groups = lax.axis_size("grp")
    members = lax.axis_size("feat")
    count, depth = points.shape
    samples = dual_weights.shape[1]
    features = frequencies.shape[1]
    scales = (1.0 / math.sqrt(count * groups * members), signal * math.sqrt(2.0 / (features * members)))
    tiles = batch_tiles.reshape(2)
    observed = observed.reshape(1, count)
    phases = phases.reshape(1, features)
    points, duals, velocity, noise, weights = (a.T for a in (points, dual_weights, velocity, noise_draws, prior_weights))
    part = (samples, TILE)

    def other_core(array):
        return swap(array, groups, members, 0, 1)

    def other_chips(array):
        return [swap(array, groups, members, 0, 2 * k + 1) for k in range(1, members // 2)]

    def other_groups(array):
        return [swap(array, groups, members, k, 1) for k in range(1, groups)]

    whole = (samples, count)
    other_points = other_core(points)
    marks, static = call(
        place_kernel, [((32, count), f32), ((samples + depth, count), bf16)], tiles, points, duals,
        name="place", from_hbm=(0, 1, 2), scratch_for=(0, 1, 2), flops=PLACE,
    )
    fixed = [static, swap(static, groups, members, 1, 1)]
    (batch,) = call(pack_kernel, [((2 * depth, TILE), bf16)], marks, static, other_points, name="pack", flops=PACK)
    angles, weights, base, velocity, duals = call(
        prepare_kernel,
        [((ANGLE_ROWS, features), bf16), ((samples, features), bf16), ((2 * samples, TILE), f32), (whole, f32), (whole, f32)],
        frequencies, phases, weights, observed, noise, velocity, duals, marks,
        name="prepare", from_hbm=(0, 1, 2, 3, 4, 5, 6), scratch_for=(0, 1, 3, 4), flops=PREPARE,
    )
    batch = [batch]
    chip_bit, group_bit = 2, 2
    while chip_bit < members or group_bit < groups:
        if group_bit < groups:
            fixed.append(swap(jnp.concatenate(fixed, axis=1), groups, members, group_bit, 1))
        if chip_bit < members:
            whole_batch = sum(batch[1:], batch[0])
            batch = [whole_batch, swap(whole_batch, groups, members, 0, members // chip_bit + 1)]
        if 2 * group_bit < groups and 2 * chip_bit < members:
            fixed[-1], batch[1] = lax.optimization_barrier((fixed[-1], batch[1]))
        chip_bit, group_bit = 2 * chip_bit, 2 * group_bit
    batch, upright, rows = call(
        stand_kernel, [((2 * depth, TILE), bf16), ((2 * TILE, ANGLE_ROWS), bf16), ((2 * TILE, depth), f32)], *batch,
        name="stand",
    )
    share, send = call(
        functools.partial(first_kernel, scales), [(part, f32), ((samples + depth, TILE), bf16)],
        angles, weights, base, batch, upright, rows, *fixed, flops=10**9, name="first",
    )
    moves = [send] + other_groups(send)
    (later,) = call(
        functools.partial(second_kernel, scales), [(part, f32)], angles, weights, base, upright, rows, *fixed,
        flops=10**9, name="second",
    )
    (total,) = call(
        functools.partial(correct_kernel, scales), [((2 * samples, TILE), f32)],
        rows, share, later, *moves, flops=10**8, name="correct",
    )
    total = total + other_core(total)
    bit = 2
    while bit < members:
        total = total + swap((total * SHRINK).astype(jnp.float16), groups, members, 0, bit + 1).astype(f32) * (1.0 / SHRINK)
        bit *= 2
    new_duals, new_velocity = call(
        finish_kernel, [(whole, f32)] * 2, marks, total, duals, velocity, name="finish"
    )
    return new_duals.T, new_velocity.T


def solution(mesh):
    return jax.shard_map(
        local,
        mesh=mesh,
        in_specs=(
            P(("grp", "feat"), None),
            P(("grp", "feat"), None),
            P(("grp", "feat"), None),
            P(("grp", "feat")),
            P(("grp", "feat"), None),
            P(None, "feat"),
            P("feat"),
            P("feat", None),
            P(None, "grp", None),
        ),
        out_specs=(P(("grp", "feat"), None), P(("grp", "feat"), None)),
        check_vma=False,
    )
```

```python
import functools
import math

import jax
import jax.numpy as jnp
import numpy as np
from jax import lax
from jax.experimental import pallas as pl
from jax.experimental.pallas import tpu as pltpu
from jax.sharding import PartitionSpec as P

TILE = 128
CHUNK = 256

amplitude = 4.0
signal = 2.0
momentum = 0.9
step_size = 0.5

f32 = jnp.float32
bf16 = jnp.bfloat16

SHRINK = 0.25

def cos_terms():
    nodes = np.cos(np.pi * (np.arange(64) + 0.5) / 64)
    squares = (nodes + 1.0) * 0.125
    fit = np.polynomial.chebyshev.Chebyshev.fit(
        squares, np.cos(2.0 * np.pi * np.sqrt(squares)), 5, domain=[0.0, 0.25]
    )
    return [float(c) for c in fit.convert(kind=np.polynomial.Polynomial).coef]


COS = cos_terms()
ANGLE_ROWS = 128


def cosine(turns):
    rest = turns - jnp.round(turns)
    square = rest * rest
    total = COS[-1] * square + COS[-2]
    for term in COS[-3::-1]:
        total = total * square + term
    return total


def three_parts(wide):
    high = wide.astype(bf16)
    rest = wide - high.astype(f32)
    middle = rest.astype(bf16)
    return high, middle, (rest - middle.astype(f32)).astype(bf16)


def rows_of(turned):
    wide = turned.astype(f32)
    depth, tile = wide.shape
    ids = lax.broadcasted_iota(jnp.int32, (ANGLE_ROWS - 3 * depth, tile), 0)
    upright = jnp.concatenate([wide, wide, wide, jnp.where(ids < 3, 1.0, 0.0)], axis=0).T
    return upright.astype(bf16), upright[:, :depth]


def across(left, right):
    return lax.dot_general(left, right, (((1,), (1,)), ((), ())), preferred_element_type=f32)


def kernel_sum(rows, blocks, depth):
    rows_bf = rows.astype(bf16)
    scale = -math.log2(math.e) / depth
    row_part = jnp.sum(rows * rows, axis=1, keepdims=True) * scale + math.log2(amplitude)
    total = None
    for block_ref in blocks:
        values = block_ref.shape[0] - depth
        size = block_ref.shape[1]
        step = min(size, CHUNK)
        for start in range(0, size, step):
            cut = slice(start, start + step)
            points = block_ref[values:, cut]
            wide = points.astype(f32)
            norm_part = jnp.sum(wide * wide, axis=0, keepdims=True) * scale
            inner = jnp.dot(rows_bf, points, preferred_element_type=f32)
            kern = jnp.exp2(inner * (-2.0 * scale) + (row_part + norm_part)).astype(bf16)
            part = across(block_ref[:values, cut], kern)
            total = part if total is None else total + part
    return total


def prior_sum(upright, angle_ref, weight_ref):
    total = None
    for start in range(0, angle_ref.shape[1], CHUNK):
        cut = slice(start, start + CHUNK)
        turns = jnp.dot(upright, angle_ref[:, cut], preferred_element_type=f32)
        part = across(weight_ref[:, cut], cosine(turns).astype(bf16))
        total = part if total is None else total + part
    return total


PLACE, PACK, PREPARE, JOIN = 2 * 10**9, 10**9, 10**9, 3 * 10**9


def place_of(tiles_ref, step, tiles_per, core=0):
    tile = tiles_ref[step]
    mine = lax.div(tile, tiles_per) == lax.bitwise_xor(lax.axis_index("feat"), core)
    return mine, pl.ds(pl.multiple_of(lax.rem(tile, tiles_per) * TILE, TILE), TILE)


def fetch(pairs, sems):
    copies = [pltpu.make_async_copy(src, dst, sems.at[k]) for k, (src, dst) in enumerate(pairs)]
    for copy in copies:
        copy.start()
    for copy in copies:
        copy.wait()


def place_kernel(tiles_hbm, points_hbm, duals_hbm, marks_ref, static_ref, tiles_ref, points_ref, duals_ref, sems):
    fetch([(tiles_hbm, tiles_ref), (points_hbm, points_ref), (duals_hbm, duals_ref)], sems)
    count = points_ref.shape[1]
    values = duals_ref.shape[0]
    columns = lax.broadcasted_iota(jnp.int32, (8, count), 1)
    for core in range(2):
        for step in range(2):
            mine, where = place_of(tiles_ref, step, count // TILE, core)
            inside = (columns >= where.start) & (columns < where.start + TILE)
            row = 8 * (step + 2 * core)
            marks_ref[row : row + 8, :] = jnp.where(mine & inside, 1.0, 0.0)
    static_ref[:values, :] = duals_ref[...].astype(bf16)
    static_ref[values:, :] = points_ref[...]


def pack_kernel(marks_ref, static_ref, other_ref, batch_ref):
    depth, count = other_ref.shape
    values = static_ref.shape[0] - depth
    for step in range(2):
        rows = None
        for core, points in enumerate((static_ref[values:, :], other_ref[...])):
            row = 8 * (step + 2 * core)
            kept = jnp.where(marks_ref[row : row + 1, :] > 0.0, points.astype(f32), 0.0)
            for start in range(0, count, TILE):
                piece = kept[:, start : start + TILE]
                rows = piece if rows is None else rows + piece
        batch_ref[depth * step : depth * (step + 1), :] = rows.astype(bf16)


def prepare_kernel(
    freq_hbm, phase_hbm, weight_hbm, observed_hbm, noise_hbm, velocity_hbm, duals_hbm, marks_ref,
    angle_ref, weight_ref, base_ref, velocity_ref, duals_ref,
    freq_ref, phase_ref, observed_ref, noise_ref, sems,
):
    fetch(
        [
            (freq_hbm, freq_ref), (phase_hbm, phase_ref), (weight_hbm, weight_ref),
            (observed_hbm, observed_ref), (noise_hbm, noise_ref), (velocity_hbm, velocity_ref), (duals_hbm, duals_ref),
        ],
        sems,
    )
    depth, count = freq_ref.shape
    a_turn = 0.5 / math.pi
    for k, part in enumerate(three_parts(freq_ref[...].astype(f32) * a_turn)):
        angle_ref[depth * k : depth * (k + 1), :] = part
    pad = ANGLE_ROWS - 3 * depth
    ids = lax.broadcasted_iota(jnp.int32, (pad, count), 0)
    tail = jnp.zeros((pad, count), f32)
    for k, part in enumerate(three_parts(phase_ref[...] * a_turn)):
        tail = jnp.where(ids == k, part.astype(f32), tail)
    angle_ref[3 * depth :, :] = tail.astype(bf16)

    values, count = velocity_ref.shape
    data = step_size * (observed_ref[...] - noise_ref[...])
    for step in range(2):
        here = data + momentum * velocity_ref[...] if step == 0 else data
        here = jnp.where(marks_ref[8 * step : 8 * step + 1, :] > 0.0, here, 0.0)
        share = here[:, :TILE]
        for start in range(TILE, count, TILE):
            share = share + here[:, start : start + TILE]
        base_ref[values * step : values * (step + 1), :] = share


def stand_kernel(*refs):
    terms, (batch_ref, upright_ref, rows_ref) = refs[:-3], refs[-3:]
    batch = terms[0][...]
    for term_ref in terms[1:]:
        batch = batch + term_ref[...]
    batch_ref[...] = batch
    depth = batch.shape[0] // 2
    for step in range(2):
        upright, rows = rows_of(batch[depth * step : depth * (step + 1)])
        upright_ref[TILE * step : TILE * (step + 1), :] = upright
        rows_ref[TILE * step : TILE * (step + 1), :] = rows


def share_of(scales, step, upright_ref, rows_ref, angle_ref, weight_ref, base_ref, blocks):
    inv_root, prior_scale = scales
    cut = slice(TILE * step, TILE * (step + 1))
    rows = rows_ref[cut, :]
    kernel_part = kernel_sum(rows, blocks, rows.shape[1])
    prior_part = prior_sum(upright_ref[cut, :], angle_ref, weight_ref)
    values = prior_part.shape[0]
    base = base_ref[values * step : values * (step + 1), :]
    return base - (step_size * inv_root) * kernel_part - (step_size * prior_scale) * prior_part


def first_kernel(scales, angle_ref, weight_ref, base_ref, batch_ref, upright_ref, rows_ref, *rest):
    blocks, (share_ref, send_ref) = rest[:-2], rest[-2:]
    share = share_of(scales, 0, upright_ref, rows_ref, angle_ref, weight_ref, base_ref, blocks)
    share_ref[...] = share
    send_ref[: share.shape[0], :] = share.astype(bf16)
    send_ref[share.shape[0] :, :] = batch_ref[: batch_ref.shape[0] // 2, :]


def second_kernel(scales, angle_ref, weight_ref, base_ref, upright_ref, rows_ref, *rest):
    blocks, share_ref = rest[:-1], rest[-1]
    share_ref[...] = share_of(scales, 1, upright_ref, rows_ref, angle_ref, weight_ref, base_ref, blocks)


def correct_kernel(scales, rows_ref, second_ref, *rest):
    blocks, new_ref = rest[:-1], rest[-1]
    rows = rows_ref[TILE:, :]
    new_ref[...] = second_ref[...] - (step_size * scales[0]) * kernel_sum(rows, blocks, rows.shape[1])


def join_kernel(scales, rows_ref, block_ref, new_ref):
    rows = rows_ref[TILE:, :]
    new_ref[...] = (-step_size * scales[0]) * kernel_sum(rows, (block_ref,), rows.shape[1])


def finish_kernel(marks_ref, total_ref, duals_ref, velocity_ref, new_duals_ref, new_velocity_ref):
    values, count = duals_ref.shape
    repeats = count // TILE
    total = jnp.concatenate([total_ref[...]] * repeats, axis=1)
    first, second = marks_ref[0:1, :] > 0.0, marks_ref[8:9, :] > 0.0
    velocity, duals = velocity_ref[...], duals_ref[...]
    moved = total[:values, :]
    velocity = jnp.where(first, moved, velocity)
    duals = jnp.where(first, duals + moved, duals)
    moved = momentum * velocity + total[values:, :]
    new_velocity_ref[...] = jnp.where(second, moved, velocity)
    new_duals_ref[...] = jnp.where(second, duals + moved, duals)


def call(kernel, outs, *args, flops=0, name=None, from_hbm=(), scratch_for=()):
    args = [pltpu.with_memory_space_constraint(a, pltpu.HBM) if k in from_hbm else a for k, a in enumerate(args)]
    scratch = [(pltpu.SMEM if args[k].dtype == jnp.int32 else pltpu.VMEM)(args[k].shape, args[k].dtype) for k in scratch_for]
    if from_hbm:
        scratch.append(pltpu.SemaphoreType.DMA((len(from_hbm),)))
    return pl.pallas_call(
        kernel,
        out_shape=[jax.ShapeDtypeStruct(shape, dtype) for shape, dtype in outs],
        in_specs=[pl.BlockSpec(memory_space=pltpu.HBM if k in from_hbm else pltpu.VMEM) for k in range(len(args))],
        out_specs=[pl.BlockSpec(memory_space=pltpu.VMEM)] * len(outs),
        scratch_shapes=scratch,
        compiler_params=pltpu.CompilerParams(vmem_limit_bytes=24 * 1024 * 1024),
        cost_estimate=pl.CostEstimate(
            flops=flops,
            bytes_accessed=0 if flops == 0 else sum(a.size * a.dtype.itemsize for a in args),
            transcendentals=0,
        ),
        name=name,
    )(*args)


def swap(array, groups, members, group_bits, member_bits):
    pairs = [
        (g * members + m, (g ^ group_bits) * members + (m ^ member_bits)) for g in range(groups) for m in range(members)
    ]
    return lax.ppermute(array, ("grp", "feat"), pairs)


def local(points, dual_weights, velocity, observed, noise_draws, frequencies, phases, prior_weights, batch_tiles):
    groups = lax.axis_size("grp")
    members = lax.axis_size("feat")
    count, depth = points.shape
    samples = dual_weights.shape[1]
    features = frequencies.shape[1]
    scales = (1.0 / math.sqrt(count * groups * members), signal * math.sqrt(2.0 / (features * members)))
    tiles = batch_tiles.reshape(2)
    observed = observed.reshape(1, count)
    phases = phases.reshape(1, features)
    points, duals, velocity, noise, weights = (a.T for a in (points, dual_weights, velocity, noise_draws, prior_weights))
    part = (samples, TILE)

    def other_core(array):
        return swap(array, groups, members, 0, 1)

    def other_chips(array):
        return [swap(array, groups, members, 0, 2 * k + 1) for k in range(1, members // 2)]

    def other_groups(array):
        return [swap(array, groups, members, k, 1) for k in range(1, groups)]

    whole = (samples, count)
    other_points = other_core(points)
    marks, static = call(
        place_kernel, [((32, count), f32), ((samples + depth, count), bf16)], tiles, points, duals,
        name="place", from_hbm=(0, 1, 2), scratch_for=(0, 1, 2), flops=PLACE,
    )
    fixed = [static, swap(static, groups, members, 1, 1)]
    (batch,) = call(pack_kernel, [((2 * depth, TILE), bf16)], marks, static, other_points, name="pack", flops=PACK)
    angles, weights, base, velocity, duals = call(
        prepare_kernel,
        [((ANGLE_ROWS, features), bf16), ((samples, features), bf16), ((2 * samples, TILE), f32), (whole, f32), (whole, f32)],
        frequencies, phases, weights, observed, noise, velocity, duals, marks,
        name="prepare", from_hbm=(0, 1, 2, 3, 4, 5, 6), scratch_for=(0, 1, 3, 4), flops=PREPARE,
    )
    batch = [batch]
    chip_bit, group_bit = 2, 2
    while chip_bit < members or group_bit < groups:
        if group_bit < groups:
            fixed.append(swap(jnp.concatenate(fixed, axis=1), groups, members, group_bit, 1))
        if chip_bit < members:
            whole_batch = sum(batch[1:], batch[0])
            batch = [whole_batch, swap(whole_batch, groups, members, 0, members // chip_bit + 1)]
        if 2 * group_bit < groups and 2 * chip_bit < members:
            fixed[-1], batch[1] = lax.optimization_barrier((fixed[-1], batch[1]))
        chip_bit, group_bit = 2 * chip_bit, 2 * group_bit
    batch, upright, rows = call(
        stand_kernel, [((2 * depth, TILE), bf16), ((2 * TILE, ANGLE_ROWS), bf16), ((2 * TILE, depth), f32)], *batch,
        name="stand",
    )
    share, send = call(
        functools.partial(first_kernel, scales), [(part, f32), ((samples + depth, TILE), bf16)],
        angles, weights, base, batch, upright, rows, *fixed, flops=10**9, name="first",
    )
    summed = other_core(share)
    moves = [send] + other_groups(send)[:-1]
    share = share + summed
    last = jnp.concatenate([share.astype(bf16), batch[:depth]], axis=0)
    last, upright = lax.optimization_barrier((last, upright))
    last = swap(last, groups, members, groups - 1, 1)
    (later,) = call(
        functools.partial(second_kernel, scales), [(part, f32)], angles, weights, base, upright, rows, *fixed,
        flops=0, name="second",
    )
    (later,) = call(
        functools.partial(correct_kernel, scales), [(part, f32)], rows, later, *moves, flops=0, name="correct"
    )
    other = other_core((later * SHRINK).astype(jnp.float16)).astype(f32) * (1.0 / SHRINK)
    (joined,) = call(
        functools.partial(join_kernel, scales), [(part, f32)], rows, last, flops=JOIN, name="join"
    )
    total = jnp.concatenate([share, later + other + joined], axis=0)
    bit = 2
    while bit < members:
        total = total + swap((total * SHRINK).astype(jnp.float16), groups, members, 0, bit + 1).astype(f32) * (1.0 / SHRINK)
        bit *= 2
    new_duals, new_velocity = call(
        finish_kernel, [(whole, f32)] * 2, marks, total, duals, velocity, name="finish"
    )
    return new_duals.T, new_velocity.T


def solution(mesh):
    return jax.shard_map(
        local,
        mesh=mesh,
        in_specs=(
            P(("grp", "feat"), None),
            P(("grp", "feat"), None),
            P(("grp", "feat"), None),
            P(("grp", "feat")),
            P(("grp", "feat"), None),
            P(None, "feat"),
            P("feat"),
            P("feat", None),
            P(None, "grp", None),
        ),
        out_specs=(P(("grp", "feat"), None), P(("grp", "feat"), None)),
        check_vma=False,
    )
```

```python
import functools
import math

import jax
import jax.numpy as jnp
import numpy as np
from jax import lax
from jax.experimental import pallas as pl
from jax.experimental.pallas import tpu as pltpu
from jax.sharding import PartitionSpec as P

TILE = 128
CHUNK = 256
COLUMNS = 512

amplitude = 4.0
signal = 2.0
momentum = 0.9
step_size = 0.5

f32 = jnp.float32
bf16 = jnp.bfloat16

SHRINK = 0.25


def cos_terms():
    nodes = np.cos(np.pi * (np.arange(64) + 0.5) / 64)
    squares = (nodes + 1.0) * 0.125
    fit = np.polynomial.chebyshev.Chebyshev.fit(
        squares, np.cos(2.0 * np.pi * np.sqrt(squares)), 5, domain=[0.0, 0.25]
    )
    return [float(c) for c in fit.convert(kind=np.polynomial.Polynomial).coef]


COS = cos_terms()
ANGLE_ROWS = 128


def cosine(turns):
    rest = turns - jnp.round(turns)
    square = rest * rest
    total = COS[-1] * square + COS[-2]
    for term in COS[-3::-1]:
        total = total * square + term
    return total


def three_parts(wide):
    high = wide.astype(bf16)
    rest = wide - high.astype(f32)
    middle = rest.astype(bf16)
    return high, middle, (rest - middle.astype(f32)).astype(bf16)


def rows_of(turned):
    wide = turned.astype(f32)
    depth, tile = wide.shape
    ids = lax.broadcasted_iota(jnp.int32, (ANGLE_ROWS - 3 * depth, tile), 0)
    upright = jnp.concatenate([wide, wide, wide, jnp.where(ids < 3, 1.0, 0.0)], axis=0).T
    return upright.astype(bf16), upright[:, :depth]


def across(left, right):
    return lax.dot_general(left, right, (((1,), (1,)), ((), ())), preferred_element_type=f32)


def kernel_sum(rows, blocks, depth):
    rows_bf = rows.astype(bf16)
    scale = -math.log2(math.e) / depth
    row_part = jnp.sum(rows * rows, axis=1, keepdims=True) * scale + math.log2(amplitude)
    total = None
    for block_ref in blocks:
        values = block_ref.shape[0] - depth
        size = block_ref.shape[1]
        step = min(size, COLUMNS)
        for start in range(0, size, step):
            cut = slice(start, start + step)
            points = block_ref[values:, cut]
            wide = points.astype(f32)
            norm_part = jnp.sum(wide * wide, axis=0, keepdims=True) * scale
            inner = jnp.dot(rows_bf, points, preferred_element_type=f32)
            kern = jnp.exp2(inner * (-2.0 * scale) + (row_part + norm_part)).astype(bf16)
            part = across(block_ref[:values, cut], kern)
            total = part if total is None else total + part
    return total


def prior_sum(upright, angle_ref, weight_ref):
    total = None
    for start in range(0, angle_ref.shape[1], CHUNK):
        cut = slice(start, start + CHUNK)
        turns = jnp.dot(upright, angle_ref[:, cut], preferred_element_type=f32)
        part = across(weight_ref[:, cut], cosine(turns).astype(bf16))
        total = part if total is None else total + part
    return total


PLACE, PACK, PREPARE, JOIN = 2 * 10**9, 10**9, 10**9, 3 * 10**9


def fetch(pairs, sems):
    copies = [pltpu.make_async_copy(src, dst, sems.at[k]) for k, (src, dst) in enumerate(pairs)]
    for copy in copies:
        copy.start()
    for copy in copies:
        copy.wait()


def place_kernel(tiles_hbm, points_hbm, duals_hbm, marks_ref, static_ref, tiles_ref, points_ref, duals_ref, sems):
    fetch([(tiles_hbm, tiles_ref), (points_hbm, points_ref), (duals_hbm, duals_ref)], sems)
    count = points_ref.shape[1]
    values = duals_ref.shape[0]
    columns = lax.broadcasted_iota(jnp.int32, (8, count), 1)
    for core in range(2):
        member = lax.bitwise_xor(lax.axis_index("feat"), core)
        for step in range(2):
            place = columns + (member * count - tiles_ref[step] * TILE)
            row = 8 * (step + 2 * core)
            marks_ref[row : row + 8, :] = jnp.where((place >= 0) & (place < TILE), 1.0, 0.0)
    static_ref[:values, :] = duals_ref[...].astype(bf16)
    static_ref[values:, :] = points_ref[...]


def pack_kernel(marks_ref, static_ref, other_ref, batch_ref):
    depth, count = other_ref.shape
    values = static_ref.shape[0] - depth
    for step in range(2):
        rows = None
        for core, points in enumerate((static_ref[values:, :], other_ref[...])):
            row = 8 * (step + 2 * core)
            kept = jnp.where(marks_ref[row : row + 1, :] > 0.0, points.astype(f32), 0.0)
            for start in range(0, count, TILE):
                piece = kept[:, start : start + TILE]
                rows = piece if rows is None else rows + piece
        batch_ref[depth * step : depth * (step + 1), :] = rows.astype(bf16)


def prepare_kernel(
    freq_hbm, phase_hbm, weight_hbm, observed_hbm, noise_hbm, velocity_hbm, duals_hbm, marks_ref,
    angle_ref, weight_ref, base_ref, velocity_ref, duals_ref,
    freq_ref, phase_ref, observed_ref, noise_ref, sems,
):
    fetch(
        [
            (freq_hbm, freq_ref), (phase_hbm, phase_ref), (weight_hbm, weight_ref),
            (observed_hbm, observed_ref), (noise_hbm, noise_ref), (velocity_hbm, velocity_ref), (duals_hbm, duals_ref),
        ],
        sems,
    )
    depth, count = freq_ref.shape
    a_turn = 0.5 / math.pi
    for k, part in enumerate(three_parts(freq_ref[...].astype(f32) * a_turn)):
        angle_ref[depth * k : depth * (k + 1), :] = part
    pad = ANGLE_ROWS - 3 * depth
    ids = lax.broadcasted_iota(jnp.int32, (pad, count), 0)
    tail = jnp.zeros((pad, count), f32)
    for k, part in enumerate(three_parts(phase_ref[...] * a_turn)):
        tail = jnp.where(ids == k, part.astype(f32), tail)
    angle_ref[3 * depth :, :] = tail.astype(bf16)

    values, count = velocity_ref.shape
    data = step_size * (observed_ref[...] - noise_ref[...])
    for step in range(2):
        here = data + momentum * velocity_ref[...] if step == 0 else data
        here = jnp.where(marks_ref[8 * step : 8 * step + 1, :] > 0.0, here, 0.0)
        share = here[:, :TILE]
        for start in range(TILE, count, TILE):
            share = share + here[:, start : start + TILE]
        base_ref[values * step : values * (step + 1), :] = share


def stand_kernel(*refs):
    terms, (batch_ref, upright_ref, rows_ref) = refs[:-3], refs[-3:]
    batch = terms[0][...]
    for term_ref in terms[1:]:
        batch = batch + term_ref[...]
    batch_ref[...] = batch
    depth = batch.shape[0] // 2
    for step in range(2):
        upright, rows = rows_of(batch[depth * step : depth * (step + 1)])
        upright_ref[TILE * step : TILE * (step + 1), :] = upright
        rows_ref[TILE * step : TILE * (step + 1), :] = rows


def share_of(scales, step, upright_ref, rows_ref, angle_ref, weight_ref, base_ref, blocks):
    inv_root, prior_scale = scales
    cut = slice(TILE * step, TILE * (step + 1))
    rows = rows_ref[cut, :]
    kernel_part = kernel_sum(rows, blocks, rows.shape[1])
    prior_part = prior_sum(upright_ref[cut, :], angle_ref, weight_ref)
    values = prior_part.shape[0]
    base = base_ref[values * step : values * (step + 1), :]
    return base - (step_size * inv_root) * kernel_part - (step_size * prior_scale) * prior_part


def first_kernel(scales, angle_ref, weight_ref, base_ref, batch_ref, upright_ref, rows_ref, *rest):
    blocks, (share_ref, send_ref) = rest[:-2], rest[-2:]
    share = share_of(scales, 0, upright_ref, rows_ref, angle_ref, weight_ref, base_ref, blocks)
    share_ref[...] = share
    send_ref[: share.shape[0], :] = share.astype(bf16)
    send_ref[share.shape[0] :, :] = batch_ref[: batch_ref.shape[0] // 2, :]


def second_kernel(scales, angle_ref, weight_ref, base_ref, upright_ref, rows_ref, *rest):
    blocks, share_ref = rest[:-1], rest[-1]
    share_ref[...] = share_of(scales, 1, upright_ref, rows_ref, angle_ref, weight_ref, base_ref, blocks)


def correct_kernel(scales, rows_ref, second_ref, *rest):
    blocks, new_ref = rest[:-1], rest[-1]
    rows = rows_ref[TILE:, :]
    new_ref[...] = second_ref[...] - (step_size * scales[0]) * kernel_sum(rows, blocks, rows.shape[1])


def join_kernel(scales, rows_ref, block_ref, new_ref):
    rows = rows_ref[TILE:, :]
    new_ref[...] = (-step_size * scales[0]) * kernel_sum(rows, (block_ref,), rows.shape[1])


def finish_kernel(marks_ref, total_ref, duals_ref, velocity_ref, new_duals_ref, new_velocity_ref):
    values, count = duals_ref.shape
    repeats = count // TILE
    total = jnp.concatenate([total_ref[...]] * repeats, axis=1)
    first, second = marks_ref[0:1, :] > 0.0, marks_ref[8:9, :] > 0.0
    velocity, duals = velocity_ref[...], duals_ref[...]
    moved = total[:values, :]
    velocity = jnp.where(first, moved, velocity)
    duals = jnp.where(first, duals + moved, duals)
    moved = momentum * velocity + total[values:, :]
    new_velocity_ref[...] = jnp.where(second, moved, velocity)
    new_duals_ref[...] = jnp.where(second, duals + moved, duals)


def call(kernel, outs, *args, flops=0, name=None, from_hbm=(), scratch_for=()):
    args = [pltpu.with_memory_space_constraint(a, pltpu.HBM) if k in from_hbm else a for k, a in enumerate(args)]
    scratch = [(pltpu.SMEM if args[k].dtype == jnp.int32 else pltpu.VMEM)(args[k].shape, args[k].dtype) for k in scratch_for]
    if from_hbm:
        scratch.append(pltpu.SemaphoreType.DMA((len(from_hbm),)))
    return pl.pallas_call(
        kernel,
        out_shape=[jax.ShapeDtypeStruct(shape, dtype) for shape, dtype in outs],
        in_specs=[pl.BlockSpec(memory_space=pltpu.HBM if k in from_hbm else pltpu.VMEM) for k in range(len(args))],
        out_specs=[pl.BlockSpec(memory_space=pltpu.VMEM)] * len(outs),
        scratch_shapes=scratch,
        compiler_params=pltpu.CompilerParams(vmem_limit_bytes=24 * 1024 * 1024),
        cost_estimate=pl.CostEstimate(
            flops=flops,
            bytes_accessed=0 if flops == 0 else sum(a.size * a.dtype.itemsize for a in args),
            transcendentals=0,
        ),
        name=name,
    )(*args)


def swap(array, groups, members, group_bits, member_bits):
    pairs = [
        (g * members + m, (g ^ group_bits) * members + (m ^ member_bits)) for g in range(groups) for m in range(members)
    ]
    return lax.ppermute(array, ("grp", "feat"), pairs)


def two_ways(array, groups, members, rounds, turn):
    pairs = []
    for member in range(members):
        even = bin(member).count("1") % 2 == 0
        bit = 2 << (turn if even else rounds - 1 - turn)
        pairs += [(g * members + member, g * members + (member ^ (bit + 1))) for g in range(groups)]
    return lax.ppermute(array, ("grp", "feat"), pairs)


def local(points, dual_weights, velocity, observed, noise_draws, frequencies, phases, prior_weights, batch_tiles):
    groups = lax.axis_size("grp")
    members = lax.axis_size("feat")
    count, depth = points.shape
    samples = dual_weights.shape[1]
    features = frequencies.shape[1]
    scales = (1.0 / math.sqrt(count * groups * members), signal * math.sqrt(2.0 / (features * members)))
    tiles = batch_tiles.reshape(2)
    observed = observed.reshape(1, count)
    phases = phases.reshape(1, features)
    points, duals, velocity, noise, weights = (a.T for a in (points, dual_weights, velocity, noise_draws, prior_weights))
    part = (samples, TILE)

    def other_core(array):
        return swap(array, groups, members, 0, 1)

    def other_groups(array):
        return [swap(array, groups, members, k, 1) for k in range(1, groups)]

    whole = (samples, count)
    other_points = other_core(points)
    marks, static = call(
        place_kernel, [((32, count), f32), ((samples + depth, count), bf16)], tiles, points, duals,
        name="place", from_hbm=(0, 1, 2), scratch_for=(0, 1, 2), flops=PLACE,
    )
    fixed = [static, swap(static, groups, members, 1, 1)]
    (batch,) = call(pack_kernel, [((2 * depth, TILE), bf16)], marks, static, other_points, name="pack", flops=PACK)
    angles, weights, base, velocity, duals = call(
        prepare_kernel,
        [((ANGLE_ROWS, features), bf16), ((samples, features), bf16), ((2 * samples, TILE), f32), (whole, f32), (whole, f32)],
        frequencies, phases, weights, observed, noise, velocity, duals, marks,
        name="prepare", from_hbm=(0, 1, 2, 3, 4, 5, 6), scratch_for=(0, 1, 3, 4), flops=PREPARE,
    )
    batch = [batch]
    chip_bit, group_bit = 2, 2
    while chip_bit < members or group_bit < groups:
        if group_bit < groups:
            near = jnp.concatenate(fixed, axis=1)
            fixed = [near, swap(near, groups, members, group_bit, 1)]
        if chip_bit < members:
            whole_batch = sum(batch[1:], batch[0])
            batch = [whole_batch, swap(whole_batch, groups, members, 0, members // chip_bit + 1)]
        if 2 * group_bit < groups and 2 * chip_bit < members:
            fixed[-1], batch[1] = lax.optimization_barrier((fixed[-1], batch[1]))
        chip_bit, group_bit = 2 * chip_bit, 2 * group_bit
    batch, upright, rows = call(
        stand_kernel, [((2 * depth, TILE), bf16), ((2 * TILE, ANGLE_ROWS), bf16), ((2 * TILE, depth), f32)], *batch,
        name="stand",
    )
    share, send = call(
        functools.partial(first_kernel, scales), [(part, f32), ((samples + depth, TILE), bf16)],
        angles, weights, base, batch, upright, rows, *fixed, flops=10**9, name="first",
    )
    summed = other_core(share)
    moves = [send] + other_groups(send)[:-1]
    share = share + summed
    last = jnp.concatenate([share.astype(bf16), batch[:depth]], axis=0)
    last, upright = lax.optimization_barrier((last, upright))
    last = swap(last, groups, members, groups - 1, 1)
    (later,) = call(
        functools.partial(second_kernel, scales), [(part, f32)], angles, weights, base, upright, rows, *fixed,
        flops=0, name="second",
    )
    (later,) = call(
        functools.partial(correct_kernel, scales), [(part, f32)], rows, later, *moves, flops=0, name="correct"
    )
    other = other_core((later * SHRINK).astype(jnp.float16)).astype(f32) * (1.0 / SHRINK)
    (joined,) = call(
        functools.partial(join_kernel, scales), [(part, f32)], rows, last, flops=JOIN, name="join"
    )
    total = jnp.concatenate([share, later + other + joined], axis=0)
    rounds = members.bit_length() - 2
    for turn in range(rounds):
        small = two_ways((total * SHRINK).astype(jnp.float16), groups, members, rounds, turn)
        total = total + small.astype(f32) * (1.0 / SHRINK)
    new_duals, new_velocity = call(
        finish_kernel, [(whole, f32)] * 2, marks, total, duals, velocity, name="finish"
    )
    return new_duals.T, new_velocity.T


def solution(mesh):
    return jax.shard_map(
        local,
        mesh=mesh,
        in_specs=(
            P(("grp", "feat"), None),
            P(("grp", "feat"), None),
            P(("grp", "feat"), None),
            P(("grp", "feat")),
            P(("grp", "feat"), None),
            P(None, "feat"),
            P("feat"),
            P("feat", None),
            P(None, "grp", None),
        ),
        out_specs=(P(("grp", "feat"), None), P(("grp", "feat"), None)),
        check_vma=False,
    )
```

```python
import functools
import math

import jax
import jax.numpy as jnp
import numpy as np
from jax import lax
from jax.experimental import pallas as pl
from jax.experimental.pallas import tpu as pltpu
from jax.sharding import PartitionSpec as P

TILE = 128
CHUNK = 512
COLUMNS = 512

amplitude = 4.0
signal = 2.0
momentum = 0.9
step_size = 0.5

f32 = jnp.float32
bf16 = jnp.bfloat16

SHRINK = 0.25


def cos_terms():
    nodes = np.cos(np.pi * (np.arange(64) + 0.5) / 64)
    squares = (nodes + 1.0) * 0.125
    fit = np.polynomial.chebyshev.Chebyshev.fit(
        squares, np.cos(2.0 * np.pi * np.sqrt(squares)), 5, domain=[0.0, 0.25]
    )
    return [float(c) for c in fit.convert(kind=np.polynomial.Polynomial).coef]


COS = cos_terms()
ANGLE_ROWS = 128


def cosine(turns):
    rest = turns - jnp.round(turns)
    square = rest * rest
    total = COS[-1] * square + COS[-2]
    for term in COS[-3::-1]:
        total = total * square + term
    return total


def three_parts(wide):
    high = wide.astype(bf16)
    rest = wide - high.astype(f32)
    middle = rest.astype(bf16)
    return high, middle, (rest - middle.astype(f32)).astype(bf16)


def rows_of(turned):
    wide = turned.astype(f32)
    depth, tile = wide.shape
    ids = lax.broadcasted_iota(jnp.int32, (ANGLE_ROWS - 3 * depth, tile), 0)
    upright = jnp.concatenate([wide, wide, wide, jnp.where(ids < 3, 1.0, 0.0)], axis=0).T
    return upright.astype(bf16), upright[:, :depth]


def across(left, right):
    return lax.dot_general(left, right, (((1,), (1,)), ((), ())), preferred_element_type=f32)


def kernel_sum(rows, blocks, depth):
    rows_bf = rows.astype(bf16)
    scale = -math.log2(math.e) / depth
    row_part = jnp.sum(rows * rows, axis=1, keepdims=True) * scale + math.log2(amplitude)
    total = None
    for block_ref in blocks:
        values = block_ref.shape[0] - depth
        size = block_ref.shape[1]
        step = min(size, COLUMNS)
        for start in range(0, size, step):
            cut = slice(start, start + step)
            points = block_ref[values:, cut]
            wide = points.astype(f32)
            norm_part = jnp.sum(wide * wide, axis=0, keepdims=True) * scale
            inner = jnp.dot(rows_bf, points, preferred_element_type=f32)
            kern = jnp.exp2(inner * (-2.0 * scale) + (row_part + norm_part)).astype(bf16)
            part = across(block_ref[:values, cut], kern)
            total = part if total is None else total + part
    return total


def prior_sum(upright, angle_ref, weight_ref):
    total = None
    for start in range(0, angle_ref.shape[1], CHUNK):
        cut = slice(start, start + CHUNK)
        turns = jnp.dot(upright, angle_ref[:, cut], preferred_element_type=f32)
        part = across(weight_ref[:, cut], cosine(turns).astype(bf16))
        total = part if total is None else total + part
    return total


PLACE, PACK, PREPARE, JOIN = 2 * 10**9, 10**9, 10**9, 3 * 10**9


def fetch(pairs, sems):
    copies = [pltpu.make_async_copy(src, dst, sems.at[k]) for k, (src, dst) in enumerate(pairs)]
    for copy in copies:
        copy.start()
    for copy in copies:
        copy.wait()


def place_kernel(tiles_hbm, points_hbm, duals_hbm, marks_ref, static_ref, tiles_ref, points_ref, duals_ref, sems):
    fetch([(tiles_hbm, tiles_ref), (points_hbm, points_ref), (duals_hbm, duals_ref)], sems)
    count = points_ref.shape[1]
    values = duals_ref.shape[0]
    columns = lax.broadcasted_iota(jnp.int32, (8, count), 1)
    for core in range(2):
        member = lax.bitwise_xor(lax.axis_index("feat"), core)
        for step in range(2):
            place = columns + (member * count - tiles_ref[step] * TILE)
            row = 8 * (step + 2 * core)
            marks_ref[row : row + 8, :] = jnp.where((place >= 0) & (place < TILE), 1.0, 0.0)
    static_ref[:values, :] = duals_ref[...].astype(bf16)
    static_ref[values:, :] = points_ref[...]


def pack_kernel(marks_ref, static_ref, other_ref, batch_ref):
    depth, count = other_ref.shape
    values = static_ref.shape[0] - depth
    for step in range(2):
        rows = None
        for core, points in enumerate((static_ref[values:, :], other_ref[...])):
            row = 8 * (step + 2 * core)
            kept = jnp.where(marks_ref[row : row + 1, :] > 0.0, points.astype(f32), 0.0)
            for start in range(0, count, TILE):
                piece = kept[:, start : start + TILE]
                rows = piece if rows is None else rows + piece
        batch_ref[depth * step : depth * (step + 1), :] = rows.astype(bf16)


def prepare_kernel(
    freq_hbm, phase_hbm, weight_hbm, observed_hbm, noise_hbm, velocity_hbm, duals_hbm, marks_ref,
    angle_ref, weight_ref, base_ref, velocity_ref, duals_ref,
    freq_ref, phase_ref, observed_ref, noise_ref, sems,
):
    fetch(
        [
            (freq_hbm, freq_ref), (phase_hbm, phase_ref), (weight_hbm, weight_ref),
            (observed_hbm, observed_ref), (noise_hbm, noise_ref), (velocity_hbm, velocity_ref), (duals_hbm, duals_ref),
        ],
        sems,
    )
    depth, count = freq_ref.shape
    a_turn = 0.5 / math.pi
    for k, part in enumerate(three_parts(freq_ref[...].astype(f32) * a_turn)):
        angle_ref[depth * k : depth * (k + 1), :] = part
    pad = ANGLE_ROWS - 3 * depth
    ids = lax.broadcasted_iota(jnp.int32, (pad, count), 0)
    tail = jnp.zeros((pad, count), f32)
    for k, part in enumerate(three_parts(phase_ref[...] * a_turn)):
        tail = jnp.where(ids == k, part.astype(f32), tail)
    angle_ref[3 * depth :, :] = tail.astype(bf16)

    values, count = velocity_ref.shape
    data = step_size * (observed_ref[...] - noise_ref[...])
    for step in range(2):
        here = data + momentum * velocity_ref[...] if step == 0 else data
        here = jnp.where(marks_ref[8 * step : 8 * step + 1, :] > 0.0, here, 0.0)
        share = here[:, :TILE]
        for start in range(TILE, count, TILE):
            share = share + here[:, start : start + TILE]
        base_ref[values * step : values * (step + 1), :] = share


def stand_kernel(*refs):
    terms, (batch_ref, upright_ref, rows_ref) = refs[:-3], refs[-3:]
    batch = terms[0][...]
    for term_ref in terms[1:]:
        batch = batch + term_ref[...]
    batch_ref[...] = batch
    depth = batch.shape[0] // 2
    for step in range(2):
        upright, rows = rows_of(batch[depth * step : depth * (step + 1)])
        upright_ref[TILE * step : TILE * (step + 1), :] = upright
        rows_ref[TILE * step : TILE * (step + 1), :] = rows


def share_of(scales, step, upright_ref, rows_ref, angle_ref, weight_ref, base_ref, blocks):
    inv_root, prior_scale = scales
    cut = slice(TILE * step, TILE * (step + 1))
    rows = rows_ref[cut, :]
    kernel_part = kernel_sum(rows, blocks, rows.shape[1])
    prior_part = prior_sum(upright_ref[cut, :], angle_ref, weight_ref)
    values = prior_part.shape[0]
    base = base_ref[values * step : values * (step + 1), :]
    return base - (step_size * inv_root) * kernel_part - (step_size * prior_scale) * prior_part


def first_kernel(scales, angle_ref, weight_ref, base_ref, batch_ref, upright_ref, rows_ref, *rest):
    blocks, (share_ref, send_ref) = rest[:-2], rest[-2:]
    share = share_of(scales, 0, upright_ref, rows_ref, angle_ref, weight_ref, base_ref, blocks)
    share_ref[...] = share
    send_ref[: share.shape[0], :] = share.astype(bf16)
    send_ref[share.shape[0] :, :] = batch_ref[: batch_ref.shape[0] // 2, :]


def second_kernel(scales, angle_ref, weight_ref, base_ref, upright_ref, rows_ref, *rest):
    blocks, share_ref = rest[:-1], rest[-1]
    share_ref[...] = share_of(scales, 1, upright_ref, rows_ref, angle_ref, weight_ref, base_ref, blocks)


def correct_kernel(scales, rows_ref, second_ref, *rest):
    blocks, new_ref = rest[:-1], rest[-1]
    rows = rows_ref[TILE:, :]
    new_ref[...] = second_ref[...] - (step_size * scales[0]) * kernel_sum(rows, blocks, rows.shape[1])


def join_kernel(scales, rows_ref, *rest):
    rows = rows_ref[TILE:, :]
    blocks, new_ref = rest[:-1], rest[-1]
    new_ref[...] = (-step_size * scales[0]) * kernel_sum(rows, blocks, rows.shape[1])


def finish_kernel(marks_ref, total_ref, duals_ref, velocity_ref, new_duals_ref, new_velocity_ref):
    values, count = duals_ref.shape
    repeats = count // TILE
    total = jnp.concatenate([total_ref[...]] * repeats, axis=1)
    first, second = marks_ref[0:1, :] > 0.0, marks_ref[8:9, :] > 0.0
    velocity, duals = velocity_ref[...], duals_ref[...]
    moved = total[:values, :]
    velocity = jnp.where(first, moved, velocity)
    duals = jnp.where(first, duals + moved, duals)
    moved = momentum * velocity + total[values:, :]
    new_velocity_ref[...] = jnp.where(second, moved, velocity)
    new_duals_ref[...] = jnp.where(second, duals + moved, duals)


def call(kernel, outs, *args, flops=0, name=None, from_hbm=(), scratch_for=()):
    args = [pltpu.with_memory_space_constraint(a, pltpu.HBM) if k in from_hbm else a for k, a in enumerate(args)]
    scratch = [(pltpu.SMEM if args[k].dtype == jnp.int32 else pltpu.VMEM)(args[k].shape, args[k].dtype) for k in scratch_for]
    if from_hbm:
        scratch.append(pltpu.SemaphoreType.DMA((len(from_hbm),)))
    return pl.pallas_call(
        kernel,
        out_shape=[jax.ShapeDtypeStruct(shape, dtype) for shape, dtype in outs],
        in_specs=[pl.BlockSpec(memory_space=pltpu.HBM if k in from_hbm else pltpu.VMEM) for k in range(len(args))],
        out_specs=[pl.BlockSpec(memory_space=pltpu.VMEM)] * len(outs),
        scratch_shapes=scratch,
        compiler_params=pltpu.CompilerParams(vmem_limit_bytes=24 * 1024 * 1024),
        cost_estimate=pl.CostEstimate(
            flops=flops,
            bytes_accessed=0 if flops == 0 else sum(a.size * a.dtype.itemsize for a in args),
            transcendentals=0,
        ),
        name=name,
    )(*args)


def swap(array, groups, members, group_bits, member_bits):
    pairs = [
        (g * members + m, (g ^ group_bits) * members + (m ^ member_bits)) for g in range(groups) for m in range(members)
    ]
    return lax.ppermute(array, ("grp", "feat"), pairs)


def two_ways(array, groups, members, rounds, turn):
    pairs = []
    for member in range(members):
        even = bin(member).count("1") % 2 == 0
        bit = 2 << (turn if even else rounds - 1 - turn)
        pairs += [(g * members + member, g * members + (member ^ (bit + 1))) for g in range(groups)]
    return lax.ppermute(array, ("grp", "feat"), pairs)


def local(points, dual_weights, velocity, observed, noise_draws, frequencies, phases, prior_weights, batch_tiles):
    groups = lax.axis_size("grp")
    members = lax.axis_size("feat")
    count, depth = points.shape
    samples = dual_weights.shape[1]
    features = frequencies.shape[1]
    scales = (1.0 / math.sqrt(count * groups * members), signal * math.sqrt(2.0 / (features * members)))
    tiles = batch_tiles.reshape(2)
    observed = observed.reshape(1, count)
    phases = phases.reshape(1, features)
    points, duals, velocity, noise, weights = (a.T for a in (points, dual_weights, velocity, noise_draws, prior_weights))
    part = (samples, TILE)

    def other_core(array):
        return swap(array, groups, members, 0, 1)

    whole = (samples, count)
    other_points = other_core(points)
    marks, static = call(
        place_kernel, [((32, count), f32), ((samples + depth, count), bf16)], tiles, points, duals,
        name="place", from_hbm=(0, 1, 2), scratch_for=(0, 1, 2), flops=PLACE,
    )
    fixed = [static, swap(static, groups, members, 1, 1)]
    (batch,) = call(pack_kernel, [((2 * depth, TILE), bf16)], marks, static, other_points, name="pack", flops=PACK)
    angles, weights, base, velocity, duals = call(
        prepare_kernel,
        [((ANGLE_ROWS, features), bf16), ((samples, features), bf16), ((2 * samples, TILE), f32), (whole, f32), (whole, f32)],
        frequencies, phases, weights, observed, noise, velocity, duals, marks,
        name="prepare", from_hbm=(0, 1, 2, 3, 4, 5, 6), scratch_for=(0, 1, 3, 4), flops=PREPARE,
    )
    batch = [batch]
    chip_bit, group_bit = 2, 2
    while chip_bit < members or group_bit < groups:
        if group_bit < groups:
            near = jnp.concatenate(fixed, axis=1)
            fixed = [near, swap(near, groups, members, group_bit, 1)]
        if chip_bit < members:
            whole_batch = sum(batch[1:], batch[0])
            batch = [whole_batch, swap(whole_batch, groups, members, 0, members // chip_bit + 1)]
        if 2 * group_bit < groups and 2 * chip_bit < members:
            fixed[-1], batch[1] = lax.optimization_barrier((fixed[-1], batch[1]))
        chip_bit, group_bit = 2 * chip_bit, 2 * group_bit
    batch, upright, rows = call(
        stand_kernel, [((2 * depth, TILE), bf16), ((2 * TILE, ANGLE_ROWS), bf16), ((2 * TILE, depth), f32)], *batch,
        name="stand",
    )
    share, send = call(
        functools.partial(first_kernel, scales), [(part, f32), ((samples + depth, TILE), bf16)],
        angles, weights, base, batch, upright, rows, *fixed, flops=10**9, name="first",
    )
    summed = other_core(share)
    summed_first = [k for k in (groups - 1, groups - 2) if k > 0]
    moves = [send] + [swap(send, groups, members, k, 1) for k in range(1, groups) if k not in summed_first]
    share = share + summed
    last = jnp.concatenate([share.astype(bf16), batch[:depth]], axis=0)
    last, upright = lax.optimization_barrier((last, upright))
    last = [swap(last, groups, members, k, 1) for k in summed_first]
    (later,) = call(
        functools.partial(second_kernel, scales), [(part, f32)], angles, weights, base, upright, rows, *fixed,
        flops=0, name="second",
    )
    (later,) = call(
        functools.partial(correct_kernel, scales), [(part, f32)], rows, later, *moves, flops=0, name="correct"
    )
    other = other_core((later * SHRINK).astype(jnp.float16)).astype(f32) * (1.0 / SHRINK)
    (joined,) = call(
        functools.partial(join_kernel, scales), [(part, f32)], rows, *last, flops=JOIN, name="join"
    )
    total = jnp.concatenate([share, later + other + joined], axis=0)
    rounds = members.bit_length() - 2
    for turn in range(rounds):
        small = two_ways((total * SHRINK).astype(jnp.float16), groups, members, rounds, turn)
        total = total + small.astype(f32) * (1.0 / SHRINK)
    new_duals, new_velocity = call(
        finish_kernel, [(whole, f32)] * 2, marks, total, duals, velocity, name="finish"
    )
    return new_duals.T, new_velocity.T


def solution(mesh):
    return jax.shard_map(
        local,
        mesh=mesh,
        in_specs=(
            P(("grp", "feat"), None),
            P(("grp", "feat"), None),
            P(("grp", "feat"), None),
            P(("grp", "feat")),
            P(("grp", "feat"), None),
            P(None, "feat"),
            P("feat"),
            P("feat", None),
            P(None, "grp", None),
        ),
        out_specs=(P(("grp", "feat"), None), P(("grp", "feat"), None)),
        check_vma=False,
    )
```

```python
import functools
import math

import jax
import jax.numpy as jnp
import numpy as np
from jax import lax
from jax.experimental import pallas as pl
from jax.experimental.pallas import tpu as pltpu
from jax.sharding import PartitionSpec as P

TILE = 128
CHUNK = 512
COLUMNS = 512

amplitude = 4.0
signal = 2.0
momentum = 0.9
step_size = 0.5

f32 = jnp.float32
bf16 = jnp.bfloat16

SHRINK = 0.25


def cos_terms():
    nodes = np.cos(np.pi * (np.arange(64) + 0.5) / 64)
    squares = (nodes + 1.0) * 0.125
    fit = np.polynomial.chebyshev.Chebyshev.fit(
        squares, np.cos(2.0 * np.pi * np.sqrt(squares)), 5, domain=[0.0, 0.25]
    )
    return [float(c) for c in fit.convert(kind=np.polynomial.Polynomial).coef]


COS = cos_terms()
ANGLE_ROWS = 128


def cosine(turns):
    rest = turns - jnp.round(turns)
    square = rest * rest
    total = COS[-1] * square + COS[-2]
    for term in COS[-3::-1]:
        total = total * square + term
    return total


def three_parts(wide):
    high = wide.astype(bf16)
    rest = wide - high.astype(f32)
    middle = rest.astype(bf16)
    return high, middle, (rest - middle.astype(f32)).astype(bf16)


def rows_of(turned):
    wide = turned.astype(f32)
    depth, tile = wide.shape
    ids = lax.broadcasted_iota(jnp.int32, (ANGLE_ROWS - 3 * depth, tile), 0)
    upright = jnp.concatenate([wide, wide, wide, jnp.where(ids < 3, 1.0, 0.0)], axis=0).T
    return upright.astype(bf16), upright[:, :depth]


def across(left, right):
    return lax.dot_general(left, right, (((1,), (1,)), ((), ())), preferred_element_type=f32)


def kernel_sum(rows, blocks, depth):
    rows_bf = rows.astype(bf16)
    scale = -math.log2(math.e) / depth
    row_part = jnp.sum(rows * rows, axis=1, keepdims=True) * scale + math.log2(amplitude)
    total = None
    for block_ref in blocks:
        values = block_ref.shape[0] - depth
        size = block_ref.shape[1]
        step = min(size, COLUMNS)
        for start in range(0, size, step):
            cut = slice(start, start + step)
            points = block_ref[values:, cut]
            wide = points.astype(f32)
            norm_part = jnp.sum(wide * wide, axis=0, keepdims=True) * scale
            inner = jnp.dot(rows_bf, points, preferred_element_type=f32)
            kern = jnp.exp2(inner * (-2.0 * scale) + (row_part + norm_part)).astype(bf16)
            part = across(block_ref[:values, cut], kern)
            total = part if total is None else total + part
    return total


def prior_sum(upright, angle_ref, weight_ref):
    total = None
    for start in range(0, angle_ref.shape[1], CHUNK):
        cut = slice(start, start + CHUNK)
        turns = jnp.dot(upright, angle_ref[:, cut], preferred_element_type=f32)
        part = across(weight_ref[:, cut], cosine(turns).astype(bf16))
        total = part if total is None else total + part
    return total


PLACE, PACK, PREPARE, JOIN = 2 * 10**9, 10**9, 10**9, 3 * 10**9


def fetch(pairs, sems):
    copies = [pltpu.make_async_copy(src, dst, sems.at[k]) for k, (src, dst) in enumerate(pairs)]
    for copy in copies:
        copy.start()
    for copy in copies:
        copy.wait()


def place_kernel(tiles_hbm, points_hbm, duals_hbm, marks_ref, static_ref, tiles_ref, points_ref, duals_ref, sems):
    fetch([(tiles_hbm, tiles_ref), (points_hbm, points_ref), (duals_hbm, duals_ref)], sems)
    count = points_ref.shape[1]
    values = duals_ref.shape[0]
    columns = lax.broadcasted_iota(jnp.int32, (8, count), 1)
    for core in range(2):
        member = lax.bitwise_xor(lax.axis_index("feat"), core)
        for step in range(2):
            place = columns + (member * count - tiles_ref[step] * TILE)
            row = 8 * (step + 2 * core)
            marks_ref[row : row + 8, :] = jnp.where((place >= 0) & (place < TILE), 1.0, 0.0)
    static_ref[:values, :] = duals_ref[...].astype(bf16)
    static_ref[values:, :] = points_ref[...]


def pack_kernel(marks_ref, static_ref, other_ref, batch_ref):
    depth, count = other_ref.shape
    values = static_ref.shape[0] - depth
    for step in range(2):
        rows = None
        for core, points in enumerate((static_ref[values:, :], other_ref[...])):
            row = 8 * (step + 2 * core)
            kept = jnp.where(marks_ref[row : row + 1, :] > 0.0, points.astype(f32), 0.0)
            for start in range(0, count, TILE):
                piece = kept[:, start : start + TILE]
                rows = piece if rows is None else rows + piece
        batch_ref[depth * step : depth * (step + 1), :] = rows.astype(bf16)


def prepare_kernel(
    freq_hbm, phase_hbm, weight_hbm, observed_hbm, noise_hbm, velocity_hbm, duals_hbm, marks_ref,
    angle_ref, weight_ref, base_ref, velocity_ref, duals_ref,
    freq_ref, phase_ref, observed_ref, noise_ref, sems,
):
    fetch(
        [
            (freq_hbm, freq_ref), (phase_hbm, phase_ref), (weight_hbm, weight_ref),
            (observed_hbm, observed_ref), (noise_hbm, noise_ref), (velocity_hbm, velocity_ref), (duals_hbm, duals_ref),
        ],
        sems,
    )
    depth, count = freq_ref.shape
    a_turn = 0.5 / math.pi
    for k, part in enumerate(three_parts(freq_ref[...].astype(f32) * a_turn)):
        angle_ref[depth * k : depth * (k + 1), :] = part
    pad = ANGLE_ROWS - 3 * depth
    ids = lax.broadcasted_iota(jnp.int32, (pad, count), 0)
    tail = jnp.zeros((pad, count), f32)
    for k, part in enumerate(three_parts(phase_ref[...] * a_turn)):
        tail = jnp.where(ids == k, part.astype(f32), tail)
    angle_ref[3 * depth :, :] = tail.astype(bf16)

    values, count = velocity_ref.shape
    data = step_size * (observed_ref[...] - noise_ref[...])
    for step in range(2):
        here = data + momentum * velocity_ref[...] if step == 0 else data
        here = jnp.where(marks_ref[8 * step : 8 * step + 1, :] > 0.0, here, 0.0)
        share = here[:, :TILE]
        for start in range(TILE, count, TILE):
            share = share + here[:, start : start + TILE]
        base_ref[values * step : values * (step + 1), :] = share


def share_of(scales, step, upright, rows, angle_ref, weight_ref, base_ref, blocks):
    inv_root, prior_scale = scales
    kernel_part = kernel_sum(rows, blocks, rows.shape[1])
    prior_part = prior_sum(upright, angle_ref, weight_ref)
    values = prior_part.shape[0]
    base = base_ref[values * step : values * (step + 1), :]
    return base - (step_size * inv_root) * kernel_part - (step_size * prior_scale) * prior_part


def first_kernel(scales, parts, angle_ref, weight_ref, base_ref, *rest):
    terms, blocks, (share_ref, send_ref, batch_ref) = rest[:parts], rest[parts:-3], rest[-3:]
    batch = terms[0][...]
    for term_ref in terms[1:]:
        batch = batch + term_ref[...]
    batch_ref[...] = batch
    turned = batch[: batch.shape[0] // 2]
    upright, rows = rows_of(turned)
    share = share_of(scales, 0, upright, rows, angle_ref, weight_ref, base_ref, blocks)
    share_ref[...] = share
    send_ref[: share.shape[0], :] = share.astype(bf16)
    send_ref[share.shape[0] :, :] = turned


def second_kernel(scales, angle_ref, weight_ref, base_ref, batch_ref, *rest):
    blocks, (share_ref, rows_ref) = rest[:-2], rest[-2:]
    upright, rows = rows_of(batch_ref[batch_ref.shape[0] // 2 :, :])
    rows_ref[...] = rows
    share_ref[...] = share_of(scales, 1, upright, rows, angle_ref, weight_ref, base_ref, blocks)


def correct_kernel(scales, rows_ref, second_ref, *rest):
    blocks, new_ref = rest[:-1], rest[-1]
    rows = rows_ref[...]
    new_ref[...] = second_ref[...] - (step_size * scales[0]) * kernel_sum(rows, blocks, rows.shape[1])


def join_kernel(scales, rows_ref, *rest):
    rows = rows_ref[...]
    blocks, new_ref = rest[:-1], rest[-1]
    new_ref[...] = (-step_size * scales[0]) * kernel_sum(rows, blocks, rows.shape[1])


def finish_kernel(marks_ref, total_ref, duals_ref, velocity_ref, new_duals_ref, new_velocity_ref):
    values, count = duals_ref.shape
    repeats = count // TILE
    total = jnp.concatenate([total_ref[...]] * repeats, axis=1)
    first, second = marks_ref[0:1, :] > 0.0, marks_ref[8:9, :] > 0.0
    velocity, duals = velocity_ref[...], duals_ref[...]
    moved = total[:values, :]
    velocity = jnp.where(first, moved, velocity)
    duals = jnp.where(first, duals + moved, duals)
    moved = momentum * velocity + total[values:, :]
    new_velocity_ref[...] = jnp.where(second, moved, velocity)
    new_duals_ref[...] = jnp.where(second, duals + moved, duals)


def call(kernel, outs, *args, flops=0, name=None, from_hbm=(), scratch_for=()):
    args = [pltpu.with_memory_space_constraint(a, pltpu.HBM) if k in from_hbm else a for k, a in enumerate(args)]
    scratch = [(pltpu.SMEM if args[k].dtype == jnp.int32 else pltpu.VMEM)(args[k].shape, args[k].dtype) for k in scratch_for]
    if from_hbm:
        scratch.append(pltpu.SemaphoreType.DMA((len(from_hbm),)))
    return pl.pallas_call(
        kernel,
        out_shape=[jax.ShapeDtypeStruct(shape, dtype) for shape, dtype in outs],
        in_specs=[pl.BlockSpec(memory_space=pltpu.HBM if k in from_hbm else pltpu.VMEM) for k in range(len(args))],
        out_specs=[pl.BlockSpec(memory_space=pltpu.VMEM)] * len(outs),
        scratch_shapes=scratch,
        compiler_params=pltpu.CompilerParams(vmem_limit_bytes=24 * 1024 * 1024),
        cost_estimate=pl.CostEstimate(
            flops=flops,
            bytes_accessed=0 if flops == 0 else sum(a.size * a.dtype.itemsize for a in args),
            transcendentals=0,
        ),
        name=name,
    )(*args)


def swap(array, groups, members, group_bits, member_bits):
    pairs = [
        (g * members + m, (g ^ group_bits) * members + (m ^ member_bits)) for g in range(groups) for m in range(members)
    ]
    return lax.ppermute(array, ("grp", "feat"), pairs)


def two_ways(array, groups, members, rounds, turn):
    pairs = []
    for member in range(members):
        even = bin(member).count("1") % 2 == 0
        bit = 2 << (turn if even else rounds - 1 - turn)
        pairs += [(g * members + member, g * members + (member ^ (bit + 1))) for g in range(groups)]
    return lax.ppermute(array, ("grp", "feat"), pairs)


def local(points, dual_weights, velocity, observed, noise_draws, frequencies, phases, prior_weights, batch_tiles):
    groups = lax.axis_size("grp")
    members = lax.axis_size("feat")
    count, depth = points.shape
    samples = dual_weights.shape[1]
    features = frequencies.shape[1]
    scales = (1.0 / math.sqrt(count * groups * members), signal * math.sqrt(2.0 / (features * members)))
    tiles = batch_tiles.reshape(2)
    observed = observed.reshape(1, count)
    phases = phases.reshape(1, features)
    points, duals, velocity, noise, weights = (a.T for a in (points, dual_weights, velocity, noise_draws, prior_weights))
    part = (samples, TILE)

    def other_core(array):
        return swap(array, groups, members, 0, 1)

    whole = (samples, count)
    other_points = other_core(points)
    marks, static = call(
        place_kernel, [((32, count), f32), ((samples + depth, count), bf16)], tiles, points, duals,
        name="place", from_hbm=(0, 1, 2), scratch_for=(0, 1, 2), flops=PLACE,
    )
    fixed = [static, swap(static, groups, members, 1, 1)]
    (batch,) = call(pack_kernel, [((2 * depth, TILE), bf16)], marks, static, other_points, name="pack", flops=PACK)
    angles, weights, base, velocity, duals = call(
        prepare_kernel,
        [((ANGLE_ROWS, features), bf16), ((samples, features), bf16), ((2 * samples, TILE), f32), (whole, f32), (whole, f32)],
        frequencies, phases, weights, observed, noise, velocity, duals, marks,
        name="prepare", from_hbm=(0, 1, 2, 3, 4, 5, 6), scratch_for=(0, 1, 3, 4), flops=PREPARE,
    )
    batch = [batch]
    chip_bit, group_bit = 2, 2
    while chip_bit < members or group_bit < groups:
        if group_bit < groups:
            near = jnp.concatenate(fixed, axis=1)
            fixed = [near, swap(near, groups, members, group_bit, 1)]
        if chip_bit < members:
            whole_batch = sum(batch[1:], batch[0])
            batch = [whole_batch, swap(whole_batch, groups, members, 0, members // chip_bit + 1)]
        if 2 * group_bit < groups and 2 * chip_bit < members:
            fixed[-1], batch[1] = lax.optimization_barrier((fixed[-1], batch[1]))
        chip_bit, group_bit = 2 * chip_bit, 2 * group_bit
    share, send, batch = call(
        functools.partial(first_kernel, scales, len(batch)),
        [(part, f32), ((samples + depth, TILE), bf16), ((2 * depth, TILE), bf16)],
        angles, weights, base, *batch, *fixed, flops=10**9, name="first",
    )
    summed = other_core(share)
    summed_first = [k for k in (groups - 1, groups - 2) if k > 0]
    moves = [send] + [swap(send, groups, members, k, 1) for k in range(1, groups) if k not in summed_first]
    share = share + summed
    last = jnp.concatenate([share.astype(bf16), batch[:depth]], axis=0)
    last, batch = lax.optimization_barrier((last, batch))
    last = [swap(last, groups, members, k, 1) for k in summed_first]
    later, rows = call(
        functools.partial(second_kernel, scales), [(part, f32), ((TILE, depth), f32)],
        angles, weights, base, batch, *fixed, flops=0, name="second",
    )
    (later,) = call(
        functools.partial(correct_kernel, scales), [(part, f32)], rows, later, *moves, flops=0, name="correct"
    )
    other = other_core((later * SHRINK).astype(jnp.float16)).astype(f32) * (1.0 / SHRINK)
    (joined,) = call(
        functools.partial(join_kernel, scales), [(part, f32)], rows, *last, flops=JOIN, name="join"
    )
    total = jnp.concatenate([share, later + other + joined], axis=0)
    rounds = members.bit_length() - 2
    for turn in range(rounds):
        small = two_ways((total * SHRINK).astype(jnp.float16), groups, members, rounds, turn)
        total = total + small.astype(f32) * (1.0 / SHRINK)
    new_duals, new_velocity = call(
        finish_kernel, [(whole, f32)] * 2, marks, total, duals, velocity, name="finish"
    )
    return new_duals.T, new_velocity.T


def solution(mesh):
    return jax.shard_map(
        local,
        mesh=mesh,
        in_specs=(
            P(("grp", "feat"), None),
            P(("grp", "feat"), None),
            P(("grp", "feat"), None),
            P(("grp", "feat")),
            P(("grp", "feat"), None),
            P(None, "feat"),
            P("feat"),
            P("feat", None),
            P(None, "grp", None),
        ),
        out_specs=(P(("grp", "feat"), None), P(("grp", "feat"), None)),
        check_vma=False,
    )
```

```python
import functools
import math

import jax
import jax.numpy as jnp
import numpy as np
from jax import lax
from jax.experimental import pallas as pl
from jax.experimental.pallas import tpu as pltpu
from jax.sharding import PartitionSpec as P

TILE = 128
CHUNK = 512
COLUMNS = 512

amplitude = 4.0
signal = 2.0
momentum = 0.9
step_size = 0.5

f32 = jnp.float32
bf16 = jnp.bfloat16

SHRINK = 0.25


def cos_terms():
    nodes = np.cos(np.pi * (np.arange(64) + 0.5) / 64)
    squares = (nodes + 1.0) * 0.125
    fit = np.polynomial.chebyshev.Chebyshev.fit(
        squares, np.cos(2.0 * np.pi * np.sqrt(squares)), 5, domain=[0.0, 0.25]
    )
    return [float(c) for c in fit.convert(kind=np.polynomial.Polynomial).coef]


COS = cos_terms()
ANGLE_ROWS = 128


def cosine(turns):
    rest = turns - jnp.round(turns)
    square = rest * rest
    total = COS[-1] * square + COS[-2]
    for term in COS[-3::-1]:
        total = total * square + term
    return total


def three_parts(wide):
    high = wide.astype(bf16)
    rest = wide - high.astype(f32)
    middle = rest.astype(bf16)
    return high, middle, (rest - middle.astype(f32)).astype(bf16)


def rows_of(turned):
    wide = turned.astype(f32)
    depth, tile = wide.shape
    ids = lax.broadcasted_iota(jnp.int32, (ANGLE_ROWS - 3 * depth, tile), 0)
    upright = jnp.concatenate([wide, wide, wide, jnp.where(ids < 3, 1.0, 0.0)], axis=0).T
    return upright.astype(bf16), upright[:, :depth]


def across(left, right):
    return lax.dot_general(left, right, (((1,), (1,)), ((), ())), preferred_element_type=f32)


def kernel_sum(rows, blocks, depth):
    rows_bf = rows.astype(bf16)
    scale = -math.log2(math.e) / depth
    row_part = jnp.sum(rows * rows, axis=1, keepdims=True) * scale + math.log2(amplitude)
    blocks = [block_ref[...] for block_ref in blocks]
    if sum(block.shape[1] for block in blocks) <= COLUMNS:
        blocks = [jnp.concatenate(blocks, axis=1)]
    total = None
    for block in blocks:
        values = block.shape[0] - depth
        size = block.shape[1]
        step = min(size, COLUMNS)
        for start in range(0, size, step):
            cut = slice(start, start + step)
            points = block[values:, cut]
            wide = points.astype(f32)
            norm_part = jnp.sum(wide * wide, axis=0, keepdims=True) * scale
            inner = jnp.dot(rows_bf, points, preferred_element_type=f32)
            kern = jnp.exp2(inner * (-2.0 * scale) + (row_part + norm_part)).astype(bf16)
            part = across(block[:values, cut], kern)
            total = part if total is None else total + part
    return total


def prior_sum(upright, angle_ref, weight_ref):
    total = None
    for start in range(0, angle_ref.shape[1], CHUNK):
        cut = slice(start, start + CHUNK)
        turns = jnp.dot(upright, angle_ref[:, cut], preferred_element_type=f32)
        part = across(weight_ref[:, cut], cosine(turns).astype(bf16))
        total = part if total is None else total + part
    return total


PLACE, PACK, PREPARE, JOIN = 2 * 10**9, 10**9, 10**9, 3 * 10**9


def fetch(pairs, sems):
    copies = [pltpu.make_async_copy(src, dst, sems.at[k]) for k, (src, dst) in enumerate(pairs)]
    for copy in copies:
        copy.start()
    for copy in copies:
        copy.wait()


def place_kernel(tiles_hbm, points_hbm, duals_hbm, marks_ref, static_ref, tiles_ref, points_ref, duals_ref, sems):
    fetch([(tiles_hbm, tiles_ref), (points_hbm, points_ref), (duals_hbm, duals_ref)], sems)
    count = points_ref.shape[1]
    values = duals_ref.shape[0]
    columns = lax.broadcasted_iota(jnp.int32, (8, count), 1)
    for core in range(2):
        member = lax.bitwise_xor(lax.axis_index("feat"), core)
        for step in range(2):
            place = columns + (member * count - tiles_ref[step] * TILE)
            row = 8 * (step + 2 * core)
            marks_ref[row : row + 8, :] = jnp.where((place >= 0) & (place < TILE), 1.0, 0.0)
    static_ref[:values, :] = duals_ref[...].astype(bf16)
    static_ref[values:, :] = points_ref[...]


def pack_kernel(marks_ref, static_ref, other_ref, batch_ref):
    depth, count = other_ref.shape
    values = static_ref.shape[0] - depth
    for step in range(2):
        rows = None
        for core, points in enumerate((static_ref[values:, :], other_ref[...])):
            row = 8 * (step + 2 * core)
            kept = jnp.where(marks_ref[row : row + 1, :] > 0.0, points.astype(f32), 0.0)
            for start in range(0, count, TILE):
                piece = kept[:, start : start + TILE]
                rows = piece if rows is None else rows + piece
        batch_ref[depth * step : depth * (step + 1), :] = rows.astype(bf16)


def prepare_kernel(
    freq_hbm, phase_hbm, weight_hbm, observed_hbm, noise_hbm, velocity_hbm, duals_hbm, marks_ref,
    angle_ref, weight_ref, base_ref, velocity_ref, duals_ref,
    freq_ref, phase_ref, observed_ref, noise_ref, sems,
):
    fetch(
        [
            (freq_hbm, freq_ref), (phase_hbm, phase_ref), (weight_hbm, weight_ref),
            (observed_hbm, observed_ref), (noise_hbm, noise_ref), (velocity_hbm, velocity_ref), (duals_hbm, duals_ref),
        ],
        sems,
    )
    depth, count = freq_ref.shape
    a_turn = 0.5 / math.pi
    for k, part in enumerate(three_parts(freq_ref[...].astype(f32) * a_turn)):
        angle_ref[depth * k : depth * (k + 1), :] = part
    pad = ANGLE_ROWS - 3 * depth
    ids = lax.broadcasted_iota(jnp.int32, (pad, count), 0)
    tail = jnp.zeros((pad, count), f32)
    for k, part in enumerate(three_parts(phase_ref[...] * a_turn)):
        tail = jnp.where(ids == k, part.astype(f32), tail)
    angle_ref[3 * depth :, :] = tail.astype(bf16)

    values, count = velocity_ref.shape
    data = step_size * (observed_ref[...] - noise_ref[...])
    for step in range(2):
        here = data + momentum * velocity_ref[...] if step == 0 else data
        here = jnp.where(marks_ref[8 * step : 8 * step + 1, :] > 0.0, here, 0.0)
        share = here[:, :TILE]
        for start in range(TILE, count, TILE):
            share = share + here[:, start : start + TILE]
        base_ref[values * step : values * (step + 1), :] = share


def share_of(scales, step, upright, rows, angle_ref, weight_ref, base_ref, blocks):
    inv_root, prior_scale = scales
    prior_part = prior_sum(upright, angle_ref, weight_ref)
    kernel_part = kernel_sum(rows, blocks, rows.shape[1])
    values = prior_part.shape[0]
    base = base_ref[values * step : values * (step + 1), :]
    return base - (step_size * inv_root) * kernel_part - (step_size * prior_scale) * prior_part


def first_kernel(scales, parts, angle_ref, weight_ref, base_ref, *rest):
    terms, blocks, (share_ref, send_ref, batch_ref) = rest[:parts], rest[parts:-3], rest[-3:]
    batch = terms[0][...]
    for term_ref in terms[1:]:
        batch = batch + term_ref[...]
    batch_ref[...] = batch
    turned = batch[: batch.shape[0] // 2]
    upright, rows = rows_of(turned)
    share = share_of(scales, 0, upright, rows, angle_ref, weight_ref, base_ref, blocks)
    share_ref[...] = share
    send_ref[: share.shape[0], :] = share.astype(bf16)
    send_ref[share.shape[0] :, :] = turned


def second_kernel(scales, angle_ref, weight_ref, base_ref, batch_ref, *rest):
    blocks, (share_ref, rows_ref) = rest[:-2], rest[-2:]
    upright, rows = rows_of(batch_ref[batch_ref.shape[0] // 2 :, :])
    rows_ref[...] = rows
    share_ref[...] = share_of(scales, 1, upright, rows, angle_ref, weight_ref, base_ref, blocks)


def correct_kernel(scales, rows_ref, second_ref, *rest):
    blocks, new_ref = rest[:-1], rest[-1]
    rows = rows_ref[...]
    new_ref[...] = second_ref[...] - (step_size * scales[0]) * kernel_sum(rows, blocks, rows.shape[1])


def join_kernel(scales, rows_ref, *rest):
    rows = rows_ref[...]
    blocks, new_ref = rest[:-1], rest[-1]
    new_ref[...] = (-step_size * scales[0]) * kernel_sum(rows, blocks, rows.shape[1])


def finish_kernel(marks_ref, total_ref, duals_ref, velocity_ref, new_duals_ref, new_velocity_ref):
    values, count = duals_ref.shape
    repeats = count // TILE
    total = jnp.concatenate([total_ref[...]] * repeats, axis=1)
    first, second = marks_ref[0:1, :] > 0.0, marks_ref[8:9, :] > 0.0
    velocity, duals = velocity_ref[...], duals_ref[...]
    moved = total[:values, :]
    velocity = jnp.where(first, moved, velocity)
    duals = jnp.where(first, duals + moved, duals)
    moved = momentum * velocity + total[values:, :]
    new_velocity_ref[...] = jnp.where(second, moved, velocity)
    new_duals_ref[...] = jnp.where(second, duals + moved, duals)


def call(kernel, outs, *args, flops=0, name=None, from_hbm=(), scratch_for=()):
    args = [pltpu.with_memory_space_constraint(a, pltpu.HBM) if k in from_hbm else a for k, a in enumerate(args)]
    scratch = [(pltpu.SMEM if args[k].dtype == jnp.int32 else pltpu.VMEM)(args[k].shape, args[k].dtype) for k in scratch_for]
    if from_hbm:
        scratch.append(pltpu.SemaphoreType.DMA((len(from_hbm),)))
    return pl.pallas_call(
        kernel,
        out_shape=[jax.ShapeDtypeStruct(shape, dtype) for shape, dtype in outs],
        in_specs=[pl.BlockSpec(memory_space=pltpu.HBM if k in from_hbm else pltpu.VMEM) for k in range(len(args))],
        out_specs=[pl.BlockSpec(memory_space=pltpu.VMEM)] * len(outs),
        scratch_shapes=scratch,
        compiler_params=pltpu.CompilerParams(vmem_limit_bytes=24 * 1024 * 1024),
        cost_estimate=pl.CostEstimate(
            flops=flops,
            bytes_accessed=0 if flops == 0 else sum(a.size * a.dtype.itemsize for a in args),
            transcendentals=0,
        ),
        name=name,
    )(*args)


def swap(array, groups, members, group_bits, member_bits):
    pairs = [
        (g * members + m, (g ^ group_bits) * members + (m ^ member_bits)) for g in range(groups) for m in range(members)
    ]
    return lax.ppermute(array, ("grp", "feat"), pairs)


def two_ways(array, groups, members, rounds, turn):
    pairs = []
    for member in range(members):
        even = bin(member).count("1") % 2 == 0
        bit = 2 << (turn if even else rounds - 1 - turn)
        pairs += [(g * members + member, g * members + (member ^ (bit + 1))) for g in range(groups)]
    return lax.ppermute(array, ("grp", "feat"), pairs)


def local(points, dual_weights, velocity, observed, noise_draws, frequencies, phases, prior_weights, batch_tiles):
    groups = lax.axis_size("grp")
    members = lax.axis_size("feat")
    count, depth = points.shape
    samples = dual_weights.shape[1]
    features = frequencies.shape[1]
    scales = (1.0 / math.sqrt(count * groups * members), signal * math.sqrt(2.0 / (features * members)))
    tiles = batch_tiles.reshape(2)
    observed = observed.reshape(1, count)
    phases = phases.reshape(1, features)
    points, duals, velocity, noise, weights = (a.T for a in (points, dual_weights, velocity, noise_draws, prior_weights))
    part = (samples, TILE)

    def other_core(array):
        return swap(array, groups, members, 0, 1)

    whole = (samples, count)
    other_points = other_core(points)
    marks, static = call(
        place_kernel, [((32, count), f32), ((samples + depth, count), bf16)], tiles, points, duals,
        name="place", from_hbm=(0, 1, 2), scratch_for=(0, 1, 2), flops=PLACE,
    )
    fixed = [static, swap(static, groups, members, 1, 1)]
    (batch,) = call(pack_kernel, [((2 * depth, TILE), bf16)], marks, static, other_points, name="pack", flops=PACK)
    angles, weights, base, velocity, duals = call(
        prepare_kernel,
        [((ANGLE_ROWS, features), bf16), ((samples, features), bf16), ((2 * samples, TILE), f32), (whole, f32), (whole, f32)],
        frequencies, phases, weights, observed, noise, velocity, duals, marks,
        name="prepare", from_hbm=(0, 1, 2, 3, 4, 5, 6), scratch_for=(0, 1, 3, 4), flops=PREPARE,
    )
    batch = [batch]
    chip_bit, group_bit = 2, 2
    while chip_bit < members or group_bit < groups:
        if group_bit < groups:
            near = jnp.concatenate(fixed, axis=1)
            fixed = [near, swap(near, groups, members, group_bit, 1)]
        if chip_bit < members:
            whole_batch = sum(batch[1:], batch[0])
            batch = [whole_batch, swap(whole_batch, groups, members, 0, members // chip_bit + 1)]
        if 2 * group_bit < groups and 2 * chip_bit < members:
            fixed[-1], batch[1] = lax.optimization_barrier((fixed[-1], batch[1]))
        chip_bit, group_bit = 2 * chip_bit, 2 * group_bit
    share, send, batch = call(
        functools.partial(first_kernel, scales, len(batch)),
        [(part, f32), ((samples + depth, TILE), bf16), ((2 * depth, TILE), bf16)],
        angles, weights, base, *batch, *fixed, flops=10**9, name="first",
    )
    summed = other_core(share)
    summed_first = [k for k in (groups - 1, groups - 2) if k > 0]
    moves = [send] + [swap(send, groups, members, k, 1) for k in range(1, groups) if k not in summed_first]
    share = share + summed
    last = jnp.concatenate([share.astype(bf16), batch[:depth]], axis=0)
    last, batch = lax.optimization_barrier((last, batch))
    last = [swap(last, groups, members, k, 1) for k in summed_first]
    later, rows = call(
        functools.partial(second_kernel, scales), [(part, f32), ((TILE, depth), f32)],
        angles, weights, base, batch, *fixed, flops=0, name="second",
    )
    (later,) = call(
        functools.partial(correct_kernel, scales), [(part, f32)], rows, later, *moves, flops=0, name="correct"
    )
    other = other_core((later * SHRINK).astype(jnp.float16)).astype(f32) * (1.0 / SHRINK)
    (joined,) = call(
        functools.partial(join_kernel, scales), [(part, f32)], rows, *last, flops=JOIN, name="join"
    )
    total = jnp.concatenate([share, later + other + joined], axis=0)
    rounds = members.bit_length() - 2
    for turn in range(rounds):
        small = two_ways((total * SHRINK).astype(jnp.float16), groups, members, rounds, turn)
        total = total + small.astype(f32) * (1.0 / SHRINK)
    new_duals, new_velocity = call(
        finish_kernel, [(whole, f32)] * 2, marks, total, duals, velocity, name="finish"
    )
    return new_duals.T, new_velocity.T


def solution(mesh):
    return jax.shard_map(
        local,
        mesh=mesh,
        in_specs=(
            P(("grp", "feat"), None),
            P(("grp", "feat"), None),
            P(("grp", "feat"), None),
            P(("grp", "feat")),
            P(("grp", "feat"), None),
            P(None, "feat"),
            P("feat"),
            P("feat", None),
            P(None, "grp", None),
        ),
        out_specs=(P(("grp", "feat"), None), P(("grp", "feat"), None)),
        check_vma=False,
    )
```
